128 devices in a mesh: fsdp: 32 (over z, x, core), grp: 4 (over y).
Axes of the slice: x: 4, y: 4, z: 4, core: 2. Of those that a mesh axis runs over, the one named last changes fastest.
Arguments:
- grad: bfloat16 [64, 1024, 1024], P(None, 'fsdp')
- adam_second: float32 [64, 1024, 1024], P(None, 'fsdp', 'grp'), may hold values from 0.002 to 0.05
- left_statistic_matrix: float32 [96, 1024, 1024], P('fsdp', 'grp'), may hold values from -4 to 4
- right_statistic_matrix: float32 [96, 1024, 1024], P('fsdp', 'grp'), may hold values from -4 to 4
- left_root: bfloat16 [96, 1024, 1024], P('fsdp', 'grp'), as said below
- right_root: bfloat16 [96, 1024, 1024], P('fsdp', 'grp'), as said below
- slot_of_block: int32 [64], replicated, may hold values from 0 to 95, as said below
Outputs:
- left_new: float32 [96, 1024, 1024], P('fsdp', 'grp')
- right_new: float32 [96, 1024, 1024], P('fsdp', 'grp')
- second_new: float32 [64, 1024, 1024], P(None, 'fsdp', 'grp')
- direction: float32 [64, 1024, 1024], P(None, 'fsdp', 'grp')
The draws below stay inside these ranges and needn't reach their ends.
Inputs may be any that keep to these rules, and one draw needn't show every extreme that they name: `slot_of_block`: entries are distinct. Slot s belongs to the owner s // 3 along fsdp; some owner has all 3 of its slots named. `left_root`: each slot's matrix is symmetric. `right_root`: each slot's matrix is symmetric.
All inputs are finite; a program needn't handle non-finite values.
Results may differ from the reference program's by a relative error of at most 0.0029.
Values may be sent and summed in bfloat16 or wider, within the bound.
A program may use at most 128 MiB of HBM per device.

```python
import math
import jax
import jax.numpy as jnp
from jax import lax

BLOCK_ORDER = 1024
OWNER_SLOTS = 3
GLOBAL_SLOTS = 96
NB = 64
N_FSDP = 32


def draw_grad(key, part):
    key = jax.random.fold_in(key, 11)
    random_keys = jax.random.split(key, 4)
    rows = jnp.arange(BLOCK_ORDER, dtype=jnp.float32)
    rise = 1.0 + 2.0 * rows / (BLOCK_ORDER - 1)
    base = jax.random.normal(random_keys[0], (NB, BLOCK_ORDER, BLOCK_ORDER), jnp.float32)
    row_scale = jnp.exp(jax.random.uniform(random_keys[1], (NB, BLOCK_ORDER, 1), jnp.float32) * math.log(2.0))
    col_scale = jnp.exp(jax.random.uniform(random_keys[2], (NB, 1, BLOCK_ORDER), jnp.float32) * math.log(2.0))
    scale = 0.05
    block_scale = jnp.exp(jax.random.uniform(random_keys[3], (NB, 1, 1), jnp.float32, -math.log(2.0), math.log(2.0)))
    values = base * scale * row_scale * col_scale * block_scale * rise[None, :, None]
    return values.astype(jnp.bfloat16)


def symmetric_root(key, spread_factor):
    random_keys = jax.random.split(key, 2)
    random_noise = jax.random.normal(random_keys[0], (GLOBAL_SLOTS, BLOCK_ORDER, BLOCK_ORDER), jnp.float32) * spread_factor
    random_noise = 0.5 * (random_noise + jnp.swapaxes(random_noise, 1, 2))
    diagonal_part = jax.random.uniform(random_keys[1], (GLOBAL_SLOTS, BLOCK_ORDER), jnp.float32, 0.5, 1.5)
    index = jnp.arange(BLOCK_ORDER)
    identity = (index[:, None] == index[None, :]).astype(jnp.float32)
    return (random_noise + identity[None, :, :] * diagonal_part[:, :, None]).astype(jnp.bfloat16)


def draw_left_root(key, part):
    key = jax.random.fold_in(key, 23)
    return symmetric_root(key, 0.02)


def draw_right_root(key, part):
    key = jax.random.fold_in(key, 37)
    return symmetric_root(key, 0.02)


def draw_slot_of_block(key, part):
    key = jax.random.fold_in(key, 41)
    random_keys = jax.random.split(key, 3)
    complete_owner = jax.random.randint(random_keys[0], (), 0, N_FSDP)
    owner_ranks = jax.random.permutation(random_keys[1], GLOBAL_SLOTS).astype(jnp.int32)
    owner_list = jnp.arange(GLOBAL_SLOTS, dtype=jnp.int32) // OWNER_SLOTS
    block_scores = jnp.where(owner_list == complete_owner, owner_ranks - GLOBAL_SLOTS, owner_ranks)
    chosen = jnp.argsort(block_scores, stable=True)[:NB].astype(jnp.int32)
    shuffle = jax.random.permutation(random_keys[2], NB)
    return chosen[shuffle].astype(jnp.int32)


def shard_levels(key, dims, cuts, low, high):
    level = 1.0
    for axis_at, parts in cuts:
        draws = jax.random.uniform(jax.random.fold_in(jax.random.fold_in(key, 6), axis_at), (parts,), jnp.float32, low / len(cuts), high / len(cuts))
        level = level * jnp.repeat(jnp.exp(draws), dims[axis_at] // parts).reshape((-1,) + (1,) * (len(dims) - 1 - axis_at))
    return level


def centred(key, extent, scale, bound, shards=(), kind=jnp.bfloat16):
    array = jax.random.normal(key, extent, jnp.float32) * scale
    if len(shards) > 0:
        array = shard_levels(key, extent, shards, -0.22, 0.18) * array
    return jnp.clip(array, min=-bound, max=bound).astype(kind)


def setup_inputs(seed: int = 0) -> dict:
    keys = jax.random.split(jax.random.key(seed), 8)
    return {
        "grad": draw_grad(jax.random.fold_in(keys[7], 71), 0),
        "adam_second": jnp.clip(jnp.exp(math.log(0.05) - 3.218876 * jax.random.uniform(keys[1], (NB, BLOCK_ORDER, BLOCK_ORDER), jnp.float32) ** shard_levels(keys[1], (NB, BLOCK_ORDER, BLOCK_ORDER), ((1, 32), (2, 4)), -0.2, 0.2)), 0.002, 0.05),
        "left_statistic_matrix": centred(keys[2], (GLOBAL_SLOTS, BLOCK_ORDER, BLOCK_ORDER), 0.5, 4.0, ((0, 32), (1, 4)), jnp.float32),
        "right_statistic_matrix": centred(keys[3], (GLOBAL_SLOTS, BLOCK_ORDER, BLOCK_ORDER), 0.5, 4.0, ((0, 32), (1, 4)), jnp.float32),
        "left_root": draw_left_root(jax.random.fold_in(keys[7], 71), 0),
        "right_root": draw_right_root(jax.random.fold_in(keys[7], 71), 0),
        "slot_of_block": draw_slot_of_block(jax.random.fold_in(keys[7], 71), 0),
    }


def reference(grad, adam_second, left_statistic_matrix, right_statistic_matrix, left_root, right_root, slot_of_block):
    wide = grad.astype(jnp.float32)
    second_new = 0.95 * adam_second + 0.05 * wide * wide
    adam = wide / (jnp.sqrt(second_new) + 1e-08)
    adam_sq = lax.optimization_barrier(jnp.mean(adam * adam, axis=(1, 2)))

    def one_block(index):
        slot = slot_of_block[index]
        block = grad[index]
        left = 0.9 * left_statistic_matrix[slot] + 0.1 * jnp.dot(block, block.T, preferred_element_type=jnp.float32)
        right = 0.9 * right_statistic_matrix[slot] + 0.1 * jnp.dot(block.T, block, preferred_element_type=jnp.float32)
        half = jnp.dot(block, right_root[slot], preferred_element_type=jnp.float32).astype(jnp.bfloat16)
        shampoo = jnp.dot(left_root[slot], half, preferred_element_type=jnp.float32)
        return (left, right, shampoo)
    lefts, rights, shampoos = lax.map(one_block, jnp.arange(NB, dtype=jnp.int32))
    left_new = (0.9 * left_statistic_matrix).at[slot_of_block].set(lefts)
    right_new = (0.9 * right_statistic_matrix).at[slot_of_block].set(rights)
    shampoo_sq = lax.optimization_barrier(jnp.mean(shampoos * shampoos, axis=(1, 2)))
    factor = jnp.sqrt(adam_sq / (shampoo_sq + 1e-06))
    direction = shampoos * factor[:, None, None]
    return (left_new, right_new, second_new, direction)
```

```python
import functools

import jax
import jax.numpy as jnp
from jax import lax
from jax.experimental import pallas as pl
from jax.experimental.pallas import tpu as pltpu
from jax.sharding import PartitionSpec as P

MESH = pl.DeviceIdType.MESH
F32, BF16 = jnp.float32, jnp.bfloat16
NT = (((1,), (1,)), ((), ()))
TN = (((0,), (0,)), ((), ()))
VMEM_LIMIT = 60 * 2**20


def exchange_kernel(
    table, grad, second, left, right, left_root, right_root,
    left_out, right_out, second_out, returned_out, sums_out,
    blocks, cols, sec, lstat, rstat, packed, whole, roots, rown, rnext, half,
    sent, handed, got, stat_out, stat_in, adam, sham, tile, tiles_in,
    sem_in, sem_g, sem_gs, sem_l, sem_ls, sem_r, sem_rs, sem_s, sem_ss, sem_h, sem_hs, sem_p, sem_ps,
    sem_t, sem_ts, sem_out,
):
    f, y = lax.axis_index("fsdp"), lax.axis_index("grp")
    c, x, z = f % 2, (f // 2) % 4, f // 8
    step = 1 - 2 * c
    up, down, across = (y + step + 4) % 4, (y - step + 4) % 4, (y + 2) % 4
    order = 1024
    share = 256
    rows = 32

    def device(zz, xx, cc):
        return zz * 8 + xx * 2 + cc

    def does(j):
        return (y + c + j) % 2 == 0

    def remote(src, dst, send, recv, ff, yy):
        return pltpu.make_async_remote_copy(
            src_ref=src, dst_ref=dst, send_sem=send, recv_sem=recv, device_id=(ff, yy), device_id_type=MESH
        )

    def wait_bytes(ref, sem):
        pltpu.make_async_copy(ref, ref, sem).wait()

    mine = pl.ds(pl.multiple_of(y * share, share), share)
    load_blocks = pltpu.make_async_copy(grad, blocks.at[pl.ds(0, 64)], sem_in.at[0])
    load_blocks.start()
    load_cols = pltpu.make_async_copy(grad.at[:, :, mine], cols, sem_in.at[1])
    load_cols.start()
    load_sec = pltpu.make_async_copy(second, sec, sem_in.at[2])
    load_sec.start()
    load_rown = pltpu.make_async_copy(right_root, rown, sem_in.at[3])
    load_rown.start()
    load_left = pltpu.make_async_copy(left, lstat, sem_in.at[4])
    load_left.start()
    load_right = pltpu.make_async_copy(right, rstat, sem_in.at[5])
    load_right.start()

    barrier = pltpu.get_barrier_semaphore()

    def greet(k, carry):
        other = (f + k) % 32
        pl.semaphore_signal(barrier, inc=1, device_id=(other, y), device_id_type=MESH)
        return carry

    lax.fori_loop(1, 32, greet, 0)
    for d in (1, 2, 3):
        pl.semaphore_signal(barrier, inc=1, device_id=(f, (y + d) % 4), device_id_type=MESH)
    blocks[64] = jnp.zeros((rows, order), BF16)
    pl.semaphore_wait(barrier, 34)

    def block_of(j, k):
        return left_root.at[j, :, pl.ds(pl.multiple_of(k * share, share), share)]

    for j in range(3):

        @pl.when(does(j))
        def _():
            remote(block_of(j, y), roots.at[j, y, y], sem_ls.at[j], sem_l.at[j], f, across).start()
            for k in range(4):
                pltpu.make_async_copy(block_of(j, k), roots.at[j, y, k], sem_l.at[j]).start()

        @pl.when(jnp.logical_not(does(j)))
        def _():
            remote(right_root.at[j], rnext.at[j], sem_rs.at[j], sem_r.at[j], f, down).start()
            for k in (y, up, across):
                remote(block_of(j, k), roots.at[j, y, k], sem_ls.at[j], sem_l.at[j], f, down).start()
            for k in (y, down):
                remote(block_of(j, k), roots.at[j, y, k], sem_ls.at[j], sem_l.at[j], f, up).start()

    load_blocks.wait()

    def send_grad(n, carry):
        j, k = n // 16, n % 16
        dz = k % 4
        dx = (k // 4 - dz + 4) % 4
        zz, xx, cc = (z + dz) % 4, (x + dx) % 4, (y + j) % 2
        ff = device(zz, xx, cc)
        packed[n] = blocks[table[ff * 3 + j]]
        target = whole.at[j, pl.ds(pl.multiple_of(f * rows, rows), rows)]

        @pl.when(ff == f)
        def _():
            pltpu.make_async_copy(packed.at[n], target, sem_g.at[j]).start()

        @pl.when(ff != f)
        def _():
            remote(packed.at[n], target, sem_gs.at[j], sem_g.at[j], ff, y).start()

        return carry

    lax.fori_loop(0, 48, send_grad, 0)

    load_cols.wait()
    load_sec.wait()
    adam[...] = jnp.zeros_like(adam)
    sham[...] = jnp.zeros_like(sham)

    def adam_block(b, carry):
        wide = cols[b].astype(F32)
        new = 0.95 * sec[b] + 0.05 * wide * wide
        sec[b] = new
        value = wide / (jnp.sqrt(new) + 1e-08)
        part = jnp.sum(value * value, axis=0, keepdims=True)
        adam[pl.ds(b, 1), :] = part[:, :128] + part[:, 128:]
        return carry

    lax.fori_loop(0, 64, adam_block, 0)
    store_sec = pltpu.make_async_copy(sec, second_out, sem_out.at[0])
    store_sec.start()
    load_rown.wait()

    def fill(j, carry):
        @pl.when(does(j))
        def _():
            wait_bytes(packed.at[pl.ds(0, 20)], sem_l.at[j])
            for r, k in ((up, y), (across, y), (down, y), (across, up), (down, up), (across, down)):
                roots[j, r, k] = roots[j, k, r].T

        return carry

    lax.fori_loop(0, 3, fill, 0)

    def spread(src, j):
        def one(k, carry):
            dz = k % 4
            dx = ((k // 4) % 4 - dz + 4) % 4
            ff = device((z + dz) % 4, (x + dx) % 4, (c + k // 16) % 2)
            piece = src.at[pl.ds(pl.multiple_of(ff * rows, rows), rows)]
            target = got.at[f * 3 + j]

            @pl.when(k == 0)
            def _():
                pltpu.make_async_copy(piece, target, sem_s).start()

            @pl.when(k != 0)
            def _():
                remote(piece, target, sem_ss.at[j], sem_s, ff, y).start()

            return carry

        lax.fori_loop(0, 32, one, 0)

    def columns(j, root, out):
        def product(r, carry):
            at = pl.ds(pl.multiple_of(r * share, share), share)
            half[r] = lax.dot_general(whole[j, at], root[j], NT, preferred_element_type=F32).astype(BF16)
            return carry

        lax.fori_loop(0, 4, product, 0)

        def outer(r, total):
            value = jnp.dot(roots[j, r, 0], half[0], preferred_element_type=F32)
            for k in range(1, 4):
                value += jnp.dot(roots[j, r, k], half[k], preferred_element_type=F32)
            out[pl.ds(pl.multiple_of(r * share, share), share), :] = value.astype(BF16)
            part = jnp.sum(value * value, axis=0, keepdims=True)
            return total + part[:, :128] + part[:, 128:]

        return lax.fori_loop(0, 4, outer, jnp.zeros((1, 128), F32))

    def direct(j, carry):
        @pl.when(does(j))
        def _():
            wait_bytes(rnext.at[j], sem_r.at[j])
            wait_bytes(whole.at[j], sem_g.at[j])
            first = columns(j, rnext, sent.at[j, 1])
            remote(sent.at[j, 1], handed.at[j], sem_hs.at[j], sem_h.at[j], f, up).start()
            other = columns(j, rown, sent.at[j, 0])
            sham[pl.ds(f * 3 + j, 1), :] = first + other
            spread(sent.at[j, 0], j)

        @pl.when(jnp.logical_not(does(j)))
        def _():
            wait_bytes(handed.at[j], sem_h.at[j])
            spread(handed.at[j], j)

        return carry

    lax.fori_loop(0, 3, direct, 0)

    tile[0] = jnp.zeros((8, 128), F32)
    tile[0, 0:1, :] = jnp.sum(adam[...].T, axis=0, keepdims=True)
    tile[0, 1:2, :] = jnp.sum(sham[...].T, axis=0, keepdims=True)
    x_peers = [(device(z, (x + d) % 4, c), y) for d in (1, 2, 3)]
    z_peers = [(device((z + d) % 4, x, c), y) for d in (1, 2, 3)]
    c_peers = [(device(z, x, 1 - c), y)]
    y_peers = [(f, (y + d) % 4) for d in (1, 2, 3)]
    stages = [x_peers, z_peers, c_peers, y_peers]

    def stage_copies(s):
        return [
            remote(tile.at[s], tiles_in.at[s, n], sem_ts.at[s, n], sem_t.at[s, n], *peer)
            for n, peer in enumerate(stages[s])
        ]

    def start_stage(s):
        for copy in stage_copies(s):
            copy.start()

    def end_stage(s):
        for copy in stage_copies(s):
            copy.wait()
        total = tile[s]
        for n in range(len(stages[s])):
            total += tiles_in[s, n]
        tile[s + 1] = total

    start_stage(0)

    load_left.wait()
    load_right.wait()

    def statistics(j, carry):
        @pl.when(does(j))
        def _():
            def rows_of(r):
                at = pl.ds(pl.multiple_of(r * share, share), share)
                lhs = whole[j, at]
                return lax.dot_general(lhs, whole[j], NT, preferred_element_type=F32)

            def cols_of(r):
                at = pl.ds(pl.multiple_of(r * share, share), share)
                lhs = whole[j, :, at].T
                return jnp.dot(lhs, whole[j], preferred_element_type=F32)

            stat_out[j, 0] = rows_of(up).astype(BF16)
            stat_out[j, 1] = cols_of(up).astype(BF16)
            remote(stat_out.at[j], stat_in.at[j], sem_ps.at[j], sem_p.at[j], f, up).start()
            lstat[j] = 0.9 * lstat[j] + 0.1 * rows_of(y)
            rstat[j] = 0.9 * rstat[j] + 0.1 * cols_of(y)

        return carry

    lax.fori_loop(0, 3, statistics, 0)
    end_stage(0)
    start_stage(1)

    def receive(j, carry):
        @pl.when(jnp.logical_not(does(j)))
        def _():
            wait_bytes(stat_in.at[j], sem_p.at[j])
            lstat[j] = 0.9 * lstat[j] + 0.1 * stat_in[j, 0].astype(F32)
            rstat[j] = 0.9 * rstat[j] + 0.1 * stat_in[j, 1].astype(F32)

        return carry

    lax.fori_loop(0, 3, receive, 0)
    store_left = pltpu.make_async_copy(lstat, left_out, sem_out.at[1])
    store_left.start()
    store_right = pltpu.make_async_copy(rstat, right_out, sem_out.at[2])
    store_right.start()
    end_stage(1)
    start_stage(2)
    end_stage(2)
    start_stage(3)
    end_stage(3)
    store_sums = pltpu.make_async_copy(tile.at[4], sums_out, sem_out.at[3])
    store_sums.start()

    for j in range(3):

        @pl.when(does(j))
        def _():
            wait_bytes(packed.at[pl.ds(0, 15)], sem_gs.at[j])
            wait_bytes(roots.at[j, 0, 0], sem_ls.at[j])
            wait_bytes(sent.at[j, 1], sem_hs.at[j])
            wait_bytes(stat_out.at[j], sem_ps.at[j])

        @pl.when(jnp.logical_not(does(j)))
        def _():
            wait_bytes(packed.at[pl.ds(0, 16)], sem_gs.at[j])
            wait_bytes(rnext.at[j], sem_rs.at[j])
            wait_bytes(packed.at[pl.ds(0, 10)], sem_ls.at[j])

        wait_bytes(got.at[pl.ds(0, 31)], sem_ss.at[j])
    wait_bytes(got, sem_s)
    store_got = pltpu.make_async_copy(got, returned_out, sem_out.at[4])
    store_got.start()
    store_got.wait()
    store_sec.wait()
    store_left.wait()
    store_right.wait()
    store_sums.wait()


def direction_kernel(slots, sums, returned, out):
    step = pl.program_id(0)
    for n in range(8):
        b = step * 8 + n
        slot = slots[b]
        adam_sq = jnp.full((1, 128), sums[0, b], F32) * (1.0 / 1048576.0)
        sham_sq = jnp.full((1, 128), sums[1, slot], F32) * (1.0 / 1048576.0)
        factor = jnp.sqrt(adam_sq / (sham_sq + 1e-06))
        wide = returned[slot].astype(F32)
        out[n, :, :128] = wide[:, :128] * factor
        out[n, :, 128:] = wide[:, 128:] * factor


def per_device(grad, second, left, right, left_root, right_root, slot_of_block):
    any_space = pl.BlockSpec(memory_space=pl.ANY)
    slots = jnp.arange(96, dtype=jnp.int32)
    named = slot_of_block[None, :] == slots[:, None]
    table = jnp.min(jnp.where(named, jnp.arange(64, dtype=jnp.int32)[None, :], 64), axis=1)
    dma = pltpu.SemaphoreType.DMA
    left_new, right_new, second_new, returned, sums = pl.pallas_call(
        exchange_kernel,
        name="exchange",
        out_shape=(
            jax.ShapeDtypeStruct((3, 256, 1024), F32),
            jax.ShapeDtypeStruct((3, 256, 1024), F32),
            jax.ShapeDtypeStruct((64, 32, 256), F32),
            jax.ShapeDtypeStruct((96, 32, 256), BF16),
            jax.ShapeDtypeStruct((8, 128), F32),
        ),
        in_specs=[pl.BlockSpec(memory_space=pltpu.SMEM)] + [any_space] * 6,
        out_specs=(any_space,) * 5,
        scratch_shapes=[
            pltpu.VMEM((65, 32, 1024), BF16),
            pltpu.VMEM((64, 32, 256), BF16),
            pltpu.VMEM((64, 32, 256), F32),
            pltpu.VMEM((3, 256, 1024), F32),
            pltpu.VMEM((3, 256, 1024), F32),
            pltpu.VMEM((48, 32, 1024), BF16),
            pltpu.VMEM((3, 1024, 1024), BF16),
            pltpu.VMEM((3, 4, 4, 256, 256), BF16),
            pltpu.VMEM((3, 256, 1024), BF16),
            pltpu.VMEM((3, 256, 1024), BF16),
            pltpu.VMEM((4, 256, 256), BF16),
            pltpu.VMEM((3, 2, 1024, 256), BF16),
            pltpu.VMEM((3, 1024, 256), BF16),
            pltpu.VMEM((96, 32, 256), BF16),
            pltpu.VMEM((3, 2, 256, 1024), BF16),
            pltpu.VMEM((3, 2, 256, 1024), BF16),
            pltpu.VMEM((128, 128), F32),
            pltpu.VMEM((128, 128), F32),
            pltpu.VMEM((5, 8, 128), F32),
            pltpu.VMEM((4, 3, 8, 128), F32),
            dma((6,)),
            dma((3,)), dma((3,)),
            dma((3,)), dma((3,)),
            dma((3,)), dma((3,)),
            dma, dma((3,)),
            dma((3,)), dma((3,)),
            dma((3,)), dma((3,)),
            dma((4, 3)), dma((4, 3)),
            dma((5,)),
        ],
        compiler_params=pltpu.CompilerParams(
            collective_id=0, has_side_effects=True, vmem_limit_bytes=VMEM_LIMIT
        ),
    )(table, grad, second, left, right, left_root, right_root)
    direction = pl.pallas_call(
        direction_kernel,
        name="direction",
        grid=(8,),
        out_shape=jax.ShapeDtypeStruct((64, 32, 256), F32),
        in_specs=[
            pl.BlockSpec(memory_space=pltpu.SMEM),
            pl.BlockSpec(memory_space=pltpu.SMEM),
            pl.BlockSpec((96, 32, 256), lambda i: (0, 0, 0)),
        ],
        out_specs=pl.BlockSpec((8, 32, 256), lambda i: (i, 0, 0)),
    )(slot_of_block, sums, returned)
    return (left_new, right_new, second_new, direction)


def solution(mesh):
    return jax.shard_map(
        per_device,
        mesh=mesh,
        in_specs=(
            P(None, "fsdp", None),
            P(None, "fsdp", "grp"),
            P("fsdp", "grp", None),
            P("fsdp", "grp", None),
            P("fsdp", "grp", None),
            P("fsdp", "grp", None),
            P(),
        ),
        out_specs=(
            P("fsdp", "grp", None),
            P("fsdp", "grp", None),
            P(None, "fsdp", "grp"),
            P(None, "fsdp", "grp"),
        ),
        check_vma=False,
    )
```

```python
import jax
import jax.numpy as jnp
from jax import lax
from jax.experimental import pallas as pl
from jax.experimental.pallas import tpu as pltpu
from jax.sharding import PartitionSpec as P

MESH = pl.DeviceIdType.MESH
F32, BF16 = jnp.float32, jnp.bfloat16
NT = (((1,), (1,)), ((), ()))
EXCHANGE_VMEM = 50 * 2**20
FINISH_VMEM = 16 * 2**20
SHARE, ROWS, ORDER = 256, 32, 1024


def exchange_kernel(
    table, grad, second, left, right, left_root, right_root,
    lstat, rstat, sec, got, sums_out,
    blocks, cols, packed, passing, whole, roots, rown, rnext, half,
    mine, give, relayed, stat_out, stat_in, adam, sham, tile, tiles_in,
    sem_in, sem_g1, sem_g1s, sem_g, sem_gs, sem_l, sem_ls, sem_r, sem_rs,
    sem_h, sem_hs, sem_s1, sem_s1s, sem_s, sem_ss, sem_p, sem_ps, sem_q, sem_qs, sem_t, sem_ts,
):
    f, y = lax.axis_index("fsdp"), lax.axis_index("grp")
    c, x, z = f % 2, (f // 2) % 4, f // 8
    across = (y + 2) % 4

    def device(zz, xx, cc):
        return zz * 8 + xx * 2 + cc

    def does(j):
        return (y + c + j) % 2 == 0

    def up(j):
        return (y + 1 if j == 0 else y + 1 + 2 * c) % 4

    def down(j):
        return (y + 3 if j == 0 else y + 3 + 2 * c) % 4

    def remote(src, dst, send, recv, ff, yy):
        return pltpu.make_async_remote_copy(
            src_ref=src, dst_ref=dst, send_sem=send, recv_sem=recv, device_id=(ff, yy), device_id_type=MESH
        )

    def move(src, dst, send, recv, ff):
        @pl.when(ff == f)
        def _():
            pltpu.make_async_copy(src, dst, recv).start()

        @pl.when(ff != f)
        def _():
            remote(src, dst, send, recv, ff, y).start()

    def wait_units(n, sem):
        ref = blocks.at[pl.ds(0, n)]
        pltpu.make_async_copy(ref, ref, sem).wait()

    def load(src, dst, n):
        copy = pltpu.make_async_copy(src, dst, sem_in.at[n])
        copy.start()
        return copy

    load_blocks = load(grad, blocks.at[pl.ds(0, 64)], 0)
    for j in range(3):
        for k in range(4):
            load(left_root.at[j, :, pl.ds(k * SHARE, SHARE)], roots.at[j * 16 + y * 4 + k], 1)
    load_rown = load(right_root, rown, 2)
    load_cols = load(grad.at[:, :, pl.ds(pl.multiple_of(y * SHARE, SHARE), SHARE)], cols, 3)
    load_sec = load(second, sec, 4)
    load_left = load(left, lstat, 5)
    load_right = load(right, rstat, 6)

    x_line = [(device(z, (x + d) % 4, c), y) for d in (1, 2, 3)]
    x_line += [(device(z, (x + d) % 4, 1 - c), y) for d in (0, 1, 2, 3)]
    z_line = [(device((z + d) % 4, x, c), y) for d in (1, 2, 3)]
    z_other = [(device((z + d) % 4, x, 1 - c), y) for d in (1, 2, 3)]
    y_line = [(f, (y + d) % 4) for d in (1, 2, 3)]
    barrier = pltpu.get_barrier_semaphore()
    for peer in x_line + z_line + z_other + y_line:
        pl.semaphore_signal(barrier, inc=1, device_id=peer, device_id_type=MESH)
    blocks[64] = jnp.zeros((ROWS, ORDER), BF16)
    pl.semaphore_wait(barrier, 16)

    def send_grad(j):
        cc = (y + j) % 2

        def pack(n, carry):
            zz, xx = n // 4, n % 4
            piece = blocks[table[device(zz, xx, cc) * 3 + j]]
            packed[0, j, xx, zz] = piece[:, :512]
            packed[1, j, zz, xx] = piece[:, 512:]
            return carry

        lax.fori_loop(0, 16, pack, 0)
        for d in (1, 3, 2):
            xx, zz = (x + d) % 4, (z + d) % 4
            remote(packed.at[0, j, xx], passing.at[0, j, x], sem_g1s.at[j], sem_g1.at[j], device(z, xx, c), y).start()
            remote(packed.at[1, j, zz], passing.at[1, j, z], sem_g1s.at[j], sem_g1.at[j], device(zz, x, c), y).start()
        pltpu.make_async_copy(packed.at[0, j, x], passing.at[0, j, x], sem_g1.at[j]).start()
        pltpu.make_async_copy(packed.at[1, j, z], passing.at[1, j, z], sem_g1.at[j]).start()

    def relay_grad(j):
        cc = (y + j) % 2
        wait_units(16, sem_g1.at[j])
        for d in (1, 3, 2, 0):
            xx, zz = (x + d) % 4, (z + d) % 4
            move(passing.at[0, j, :, zz], whole.at[j, 0, z, :, c], sem_gs.at[j], sem_g.at[j], device(zz, x, cc))
            move(passing.at[1, j, :, xx], whole.at[j, 1, :, x, c], sem_gs.at[j], sem_g.at[j], device(z, xx, cc))

    def send_roots(j):
        def block(k, yy):
            at = roots.at[j * 16 + y * 4 + k]
            remote(at, at, sem_ls.at[j], sem_l.at[j], f, yy).start()

        @pl.when(does(j))
        def _():
            block(y, across)

        @pl.when(jnp.logical_not(does(j)))
        def _():
            for k in (y, up(j), across):
                block(k, down(j))
            for k in (y, down(j)):
                block(k, up(j))
            remote(rown.at[j], rnext.at[j], sem_rs.at[j], sem_r.at[j], f, down(j)).start()

    def fill(j):
        @pl.when(does(j))
        def _():
            wait_units(12, sem_l.at[j])
            u, d, a = up(j), down(j), across
            for r, k in ((u, y), (a, y), (d, y), (a, u), (d, u), (a, d)):
                roots[j * 16 + r * 4 + k] = roots[j * 16 + k * 4 + r].T

    def rows_at(j, h, r):
        return whole[j, h, r].reshape(SHARE, 512)

    def columns(j, root, out):
        def product(r, carry):
            value = lax.dot_general(rows_at(j, 0, r), root[j, :, :512], NT, preferred_element_type=F32)
            value += lax.dot_general(rows_at(j, 1, r), root[j, :, 512:], NT, preferred_element_type=F32)
            half[r] = value.astype(BF16)
            return carry

        lax.fori_loop(0, 4, product, 0)

        def outer(r, total):
            value = jnp.dot(roots[j * 16 + r * 4], half[0], preferred_element_type=F32)
            for k in range(1, 4):
                value += jnp.dot(roots[j * 16 + r * 4 + k], half[k], preferred_element_type=F32)
            part = jnp.sum(value * value, axis=0, keepdims=True)
            out[j, 0, r] = value[:, :128].astype(BF16).reshape(4, 2, ROWS, 128)
            out[j, 1, r] = value[:, 128:].astype(BF16).reshape(4, 2, ROWS, 128)
            return total + part[:, :128] + part[:, 128:]

        return lax.fori_loop(0, 4, outer, jnp.zeros((1, 128), F32))

    def send_part(j):
        for d in (1, 3, 2):
            xx, zz = (x + d) % 4, (z + d) % 4
            remote(mine.at[j, 0, :, xx], relayed.at[0, j, x], sem_s1s.at[j], sem_s1.at[j], device(z, xx, c), y).start()
            remote(mine.at[j, 1, zz], relayed.at[1, j, z], sem_s1s.at[j], sem_s1.at[j], device(zz, x, c), y).start()
        pltpu.make_async_copy(mine.at[j, 0, :, x], relayed.at[0, j, x], sem_s1.at[j]).start()
        pltpu.make_async_copy(mine.at[j, 1, z], relayed.at[1, j, z], sem_s1.at[j]).start()

    def relay_part(j):
        wait_units(8, sem_s1.at[j])
        for d in (1, 3, 2, 0):
            xx, zz = (x + d) % 4, (z + d) % 4
            for cc in (0, 1):
                move(relayed.at[0, j, :, zz, cc], got.at[0, j, z, :, c], sem_ss.at[j], sem_s, device(zz, x, cc))
                move(relayed.at[1, j, :, xx, cc], got.at[1, j, :, x, c], sem_ss.at[j], sem_s, device(z, xx, cc))

    def direct(j):
        @pl.when(does(j))
        def _():
            wait_units(8, sem_r.at[j])
            wait_units(32, sem_g.at[j])
            first = columns(j, rnext, give)
            remote(give.at[j], mine.at[j], sem_hs.at[j], sem_h.at[j], f, up(j)).start()
            other = columns(j, rown, mine)
            sham[pl.ds(f * 3 + j, 1), :] = first + other
            send_part(j)

    def take(j):
        @pl.when(jnp.logical_not(does(j)))
        def _():
            wait_units(8, sem_h.at[j])
            send_part(j)

    def statistics(j):
        @pl.when(does(j))
        def _():
            def left_rows(r):
                value = lax.dot_general(
                    rows_at(j, 0, r), whole[j, 0].reshape(ORDER, 512), NT, preferred_element_type=F32
                )
                value += lax.dot_general(
                    rows_at(j, 1, r), whole[j, 1].reshape(ORDER, 512), NT, preferred_element_type=F32
                )
                return value

            def right_rows(r):
                at = pl.ds(pl.multiple_of((r % 2) * SHARE, SHARE), SHARE)
                lhs = whole[j, r // 2, :, :, :, :, at].reshape(ORDER, SHARE).T
                return [
                    jnp.dot(lhs, whole[j, h].reshape(ORDER, 512), preferred_element_type=F32) for h in (0, 1)
                ]

            stat_out[j, 0] = left_rows(up(j)).astype(BF16)
            remote(stat_out.at[j, 0], stat_in.at[j, 0], sem_ps.at[j], sem_p.at[j], f, up(j)).start()
            for h, value in enumerate(right_rows(down(j))):
                stat_out[j, 1, :, h * 512 : (h + 1) * 512] = value.astype(BF16)
            remote(stat_out.at[j, 1], stat_in.at[j, 1], sem_qs.at[j], sem_q.at[j], f, down(j)).start()
            lstat[j] = 0.9 * lstat[j] + 0.1 * left_rows(y)
            for h, value in enumerate(right_rows(y)):
                at = slice(h * 512, (h + 1) * 512)
                rstat[j, :, at] = 0.9 * rstat[j, :, at] + 0.1 * value

    def receive(j):
        @pl.when(jnp.logical_not(does(j)))
        def _():
            wait_units(8, sem_p.at[j])
            lstat[j] = 0.9 * lstat[j] + 0.1 * stat_in[j, 0].astype(F32)
            wait_units(8, sem_q.at[j])
            rstat[j] = 0.9 * rstat[j] + 0.1 * stat_in[j, 1].astype(F32)

    stages = [x_line, z_line, y_line]

    def stage_copies(s):
        return [
            remote(tile.at[s], tiles_in.at[s, n], sem_ts.at[s, n], sem_t.at[s, n], *peer)
            for n, peer in enumerate(stages[s])
        ]

    def start_stage(s):
        for copy in stage_copies(s):
            copy.start()

    def end_stage(s):
        for copy in stage_copies(s):
            copy.wait()
        total = tile[s]
        for n in range(len(stages[s])):
            total += tiles_in[s, n]
        tile[s + 1] = total

    load_blocks.wait()
    send_grad(0)
    wait_units(24, sem_in.at[1])
    load_rown.wait()
    send_roots(0)
    send_roots(1)
    send_grad(1)
    send_roots(2)

    load_cols.wait()
    load_sec.wait()
    adam[...] = jnp.zeros_like(adam)
    sham[...] = jnp.zeros_like(sham)

    def adam_block(b, carry):
        wide = cols[b].astype(F32)
        new = 0.95 * sec[b] + 0.05 * wide * wide
        sec[b] = new
        value = wide / (jnp.sqrt(new) + 1e-08)
        part = jnp.sum(value * value, axis=0, keepdims=True)
        adam[pl.ds(b, 1), :] = part[:, :128] + part[:, 128:]
        return carry

    lax.fori_loop(0, 64, adam_block, 0)
    load_left.wait()
    load_right.wait()

    relay_grad(0)
    send_grad(2)
    relay_grad(1)
    fill(0)
    fill(1)
    direct(0)
    relay_grad(2)
    direct(1)
    take(0)
    statistics(0)
    relay_part(0)
    fill(2)
    take(1)
    statistics(1)
    direct(2)
    relay_part(1)
    take(2)
    tile[0] = jnp.zeros((8, 128), F32)
    tile[0, 0:1, :] = jnp.sum(adam[...].T, axis=0, keepdims=True)
    tile[0, 1:2, :] = jnp.sum(sham[...].T, axis=0, keepdims=True)
    start_stage(0)
    statistics(2)
    relay_part(2)
    end_stage(0)
    start_stage(1)
    receive(0)
    receive(1)
    end_stage(1)
    start_stage(2)
    receive(2)
    end_stage(2)
    store_sums = pltpu.make_async_copy(tile.at[3], sums_out, sem_in.at[0])
    store_sums.start()

    for j in range(3):
        wait_units(12, sem_g1s.at[j])
        wait_units(6, sem_s1s.at[j])
        wait_units(7, sem_ss.at[j])

        @pl.when(does(j))
        def _():
            wait_units(12, sem_gs.at[j])
            wait_units(2, sem_ls.at[j])
            wait_units(8, sem_hs.at[j])
            wait_units(8, sem_ps.at[j])
            wait_units(8, sem_qs.at[j])

        @pl.when(jnp.logical_not(does(j)))
        def _():
            wait_units(16, sem_gs.at[j])
            wait_units(8, sem_rs.at[j])
            wait_units(10, sem_ls.at[j])

    store_sums.wait()
    wait_units(24, sem_s)


def finish_kernel(slots, sums, lstat, rstat, sec, got, left_out, right_out, second_out, out, wide, sem):
    stores = []
    for n, (src, dst) in enumerate(((lstat, left_out), (rstat, right_out), (sec, second_out))):
        copy = pltpu.make_async_copy(src, dst, sem.at[n])
        copy.start()
        stores.append(copy)

    def one(b, carry):
        slot = slots[b]
        j, owner = slot % 3, slot // 3
        c, x, z = owner % 2, (owner // 2) % 4, owner // 8
        adam_sq = jnp.full((1, 128), sums[0, b], F32) * (1.0 / 1048576.0)
        sham_sq = jnp.full((1, 128), sums[1, slot], F32) * (1.0 / 1048576.0)
        factor = jnp.sqrt(adam_sq / (sham_sq + 1e-06))
        for h in (0, 1):
            wide[b, :, h * 128 : (h + 1) * 128] = got[h, j, z, x, c].astype(F32) * factor
        return carry

    for n in range(4):
        part = pl.ds(n * 16, 16)
        lax.fori_loop(n * 16, n * 16 + 16, one, 0)
        copy = pltpu.make_async_copy(wide.at[part], out.at[part], sem.at[3 + n])
        copy.start()
        stores.append(copy)
    for copy in stores:
        copy.wait()


def per_device(grad, second, left, right, left_root, right_root, slot_of_block):
    any_space, vmem = pl.BlockSpec(memory_space=pl.ANY), pl.BlockSpec(memory_space=pltpu.VMEM)
    smem = pl.BlockSpec(memory_space=pltpu.SMEM)
    slots = jnp.arange(96, dtype=jnp.int32)
    named = slot_of_block[None, :] == slots[:, None]
    table = jnp.min(jnp.where(named, jnp.arange(64, dtype=jnp.int32)[None, :], 64), axis=1)
    dma = pltpu.SemaphoreType.DMA
    lstat, rstat, sec, got, sums = pl.pallas_call(
        exchange_kernel,
        name="exchange",
        out_shape=(
            pltpu.VMEM((3, 256, 1024), F32),
            pltpu.VMEM((3, 256, 1024), F32),
            pltpu.VMEM((64, 32, 256), F32),
            pltpu.VMEM((2, 3, 4, 4, 2, 32, 128), BF16),
            jax.ShapeDtypeStruct((8, 128), F32),
        ),
        in_specs=[smem] + [any_space] * 6,
        out_specs=(vmem,) * 4 + (any_space,),
        scratch_shapes=[
            pltpu.VMEM((65, 32, 1024), BF16),
            pltpu.VMEM((64, 32, 256), BF16),
            pltpu.VMEM((2, 3, 4, 4, 32, 512), BF16),
            pltpu.VMEM((2, 3, 4, 4, 32, 512), BF16),
            pltpu.VMEM((3, 2, 4, 4, 2, 32, 512), BF16),
            pltpu.VMEM((48, 256, 256), BF16),
            pltpu.VMEM((3, 256, 1024), BF16),
            pltpu.VMEM((3, 256, 1024), BF16),
            pltpu.VMEM((4, 256, 256), BF16),
            pltpu.VMEM((3, 2, 4, 4, 2, 32, 128), BF16),
            pltpu.VMEM((3, 2, 4, 4, 2, 32, 128), BF16),
            pltpu.VMEM((2, 3, 4, 4, 2, 32, 128), BF16),
            pltpu.VMEM((3, 2, 256, 1024), BF16),
            pltpu.VMEM((3, 2, 256, 1024), BF16),
            pltpu.VMEM((128, 128), F32),
            pltpu.VMEM((128, 128), F32),
            pltpu.VMEM((4, 8, 128), F32),
            pltpu.VMEM((3, 7, 8, 128), F32),
            dma((7,)),
            dma((3,)), dma((3,)),
            dma((3,)), dma((3,)),
            dma((3,)), dma((3,)),
            dma((3,)), dma((3,)),
            dma((3,)), dma((3,)),
            dma((3,)), dma((3,)),
            dma, dma((3,)),
            dma((3,)), dma((3,)),
            dma((3,)), dma((3,)),
            dma((3, 7)), dma((3, 7)),
        ],
        compiler_params=pltpu.CompilerParams(
            collective_id=0, has_side_effects=True, vmem_limit_bytes=EXCHANGE_VMEM
        ),
    )(table, grad, second, left, right, left_root, right_root)
    return pl.pallas_call(
        finish_kernel,
        name="finish",
        out_shape=(
            jax.ShapeDtypeStruct((3, 256, 1024), F32),
            jax.ShapeDtypeStruct((3, 256, 1024), F32),
            jax.ShapeDtypeStruct((64, 32, 256), F32),
            jax.ShapeDtypeStruct((64, 32, 256), F32),
        ),
        in_specs=[smem, smem] + [vmem] * 4,
        out_specs=(any_space,) * 4,
        scratch_shapes=[pltpu.VMEM((64, 32, 256), F32), dma((7,))],
        compiler_params=pltpu.CompilerParams(vmem_limit_bytes=FINISH_VMEM),
    )(slot_of_block, sums, lstat, rstat, sec, got)


def solution(mesh):
    return jax.shard_map(
        per_device,
        mesh=mesh,
        in_specs=(
            P(None, "fsdp", None),
            P(None, "fsdp", "grp"),
            P("fsdp", "grp", None),
            P("fsdp", "grp", None),
            P("fsdp", "grp", None),
            P("fsdp", "grp", None),
            P(),
        ),
        out_specs=(
            P("fsdp", "grp", None),
            P("fsdp", "grp", None),
            P(None, "fsdp", "grp"),
            P(None, "fsdp", "grp"),
        ),
        check_vma=False,
    )
```

```python
import jax
import jax.numpy as jnp
from jax import lax
from jax.experimental import pallas as pl
from jax.experimental.pallas import tpu as pltpu
from jax.sharding import PartitionSpec as P

MESH = pl.DeviceIdType.MESH
F32, BF16 = jnp.float32, jnp.bfloat16
NT = (((1,), (1,)), ((), ()))
EXCHANGE_VMEM = 50 * 2**20
FINISH_VMEM = 16 * 2**20
SHARE, ROWS, ORDER = 256, 32, 1024


def exchange_kernel(
    table, grad, second, left, right, left_root, right_root,
    lstat, rstat, sec, got, sums_out,
    blocks, cols, packed, passing, whole, roots, rown, rnext, half,
    mine, give, relayed, stat_out, stat_in, adam, sham, tile, tiles_in,
    sem_in, sem_g1, sem_g1s, sem_g, sem_gs, sem_l, sem_ls, sem_r, sem_rs,
    sem_os, sem_hs, sem_s1, sem_s1s, sem_s, sem_ss, sem_p, sem_ps, sem_q, sem_qs, sem_t, sem_ts,
):
    f, y = lax.axis_index("fsdp"), lax.axis_index("grp")
    c, x, z = f % 2, (f // 2) % 4, f // 8
    up, down, across = (y + 1 + 2 * c) % 4, (y + 3 + 2 * c) % 4, (y + 2) % 4

    def device(zz, xx, cc):
        return zz * 8 + xx * 2 + cc


    def remote(src, dst, send, recv, ff, yy):
        return pltpu.make_async_remote_copy(
            src_ref=src, dst_ref=dst, send_sem=send, recv_sem=recv, device_id=(ff, yy), device_id_type=MESH
        )

    def move(src, dst, send, recv, ff):
        @pl.when(ff == f)
        def _():
            pltpu.make_async_copy(src, dst, recv).start()

        @pl.when(ff != f)
        def _():
            remote(src, dst, send, recv, ff, y).start()

    def wait_bytes(ref, sem):
        pltpu.make_async_copy(ref, ref, sem).wait()

    def wait_units(n, sem):
        wait_bytes(blocks.at[pl.ds(0, n)], sem)

    def load(src, dst, n):
        copy = pltpu.make_async_copy(src, dst, sem_in.at[n])
        copy.start()
        return copy

    load_blocks = load(grad, blocks.at[pl.ds(0, 64)], 0)
    for j in range(3):
        for k in range(4):
            load(left_root.at[j, :, pl.ds(k * SHARE, SHARE)], roots.at[j * 16 + k * 4 + y], 1)
            load(right_root.at[j, :, pl.ds(k * SHARE, SHARE)], rown.at[j * 4 + k], 2)
    load_cols = load(grad.at[:, :, pl.ds(pl.multiple_of(y * SHARE, SHARE), SHARE)], cols, 3)
    load_sec = load(second, sec, 4)
    load_left = load(left, lstat, 5)
    load_right = load(right, rstat, 6)

    x_line = [(device(z, (x + d) % 4, c), y) for d in (1, 2, 3)]
    x_line += [(device(z, (x + d) % 4, 1 - c), y) for d in (0, 1, 2, 3)]
    z_line = [(device((z + d) % 4, x, c), y) for d in (1, 2, 3)]
    z_other = [(device((z + d) % 4, x, 1 - c), y) for d in (1, 2, 3)]
    y_line = [(f, (y + d) % 4) for d in (1, 2, 3)]
    senders = x_line + z_line + z_other + y_line
    for cc, yy in ((0, (y + 3) % 4), (1, (y + 1) % 4)):
        senders += [(device(z, (x + d) % 4, cc), yy) for d in (0, 1, 2, 3)]
        senders += [(device((z + d) % 4, x, cc), yy) for d in (1, 2, 3)]
    barrier = pltpu.get_barrier_semaphore()
    for peer in senders:
        pl.semaphore_signal(barrier, inc=1, device_id=peer, device_id_type=MESH)
    blocks[64] = jnp.zeros((ROWS, ORDER), BF16)
    pl.semaphore_wait(barrier, 30)

    def to_handler(j, route, piece, zs, xs, other):
        cc = (y + j) % 2
        ff = device(other, x, cc) if route == 0 else device(z, other, cc)
        move(piece, whole.at[j, route, zs, xs, c], sem_gs.at[j], sem_g.at[j], ff)

    def send_grad(j):
        cc = (y + j) % 2

        def pack(n, carry):
            zz, xx = n // 4, n % 4
            piece = blocks[table[device(zz, xx, cc) * 3 + j]]
            packed[0, j, xx, zz] = piece[:, :512]
            packed[1, j, zz, xx] = piece[:, 512:]
            return carry

        lax.fori_loop(0, 16, pack, 0)
        for d in (1, 3, 2):
            xx, zz = (x + d) % 4, (z + d) % 4
            remote(
                packed.at[0, j, xx], passing.at[0, j, x], sem_g1s.at[j], sem_g1.at[0, j, x], device(z, xx, c), y
            ).start()
            remote(
                packed.at[1, j, zz], passing.at[1, j, z], sem_g1s.at[j], sem_g1.at[1, j, z], device(zz, x, c), y
            ).start()
        for d in (1, 3, 2, 0):
            xx, zz = (x + d) % 4, (z + d) % 4
            to_handler(j, 0, packed.at[0, j, x, zz], z, x, zz)
            to_handler(j, 1, packed.at[1, j, z, xx], z, x, xx)

    def relay_grad(j):
        for e in (1, 3, 2):
            xs, zs = (x + e) % 4, (z + e) % 4
            wait_units(2, sem_g1.at[0, j, xs])
            for d in (1, 3, 2, 0):
                to_handler(j, 0, passing.at[0, j, xs, (z + d) % 4], z, xs, (z + d) % 4)
            wait_units(2, sem_g1.at[1, j, zs])
            for d in (1, 3, 2, 0):
                to_handler(j, 1, passing.at[1, j, zs, (x + d) % 4], zs, x, (x + d) % 4)

    def send_roots(j, handled):
        def block(k, yy):
            at = roots.at[j * 16 + k * 4 + y]
            remote(at, at, sem_ls.at[j], sem_l.at[j], f, yy).start()

        if handled:
            block(y, across)
        else:
            for k in (y, up, across):
                block(k, down)
                at = j * 4 + k
                remote(rown.at[at], rnext.at[at], sem_rs.at[j], sem_r.at[j], f, down).start()
            for k in (y, down):
                block(k, up)

    def fill(j):
        wait_units(12, sem_l.at[j])
        for r, k in ((up, y), (across, y), (down, y), (across, up), (down, up), (across, down)):
            roots[j * 16 + k * 4 + r] = roots[j * 16 + r * 4 + k].T
        rnext[j * 4 + y] = rown[j * 4 + up].T

    def rows_at(j, h, r):
        return whole[j, h, r].reshape(SHARE, 512)

    def direct(j):
        wait_units(6, sem_r.at[j])
        wait_units(32, sem_g.at[j])
        lhs = jnp.concatenate([whole[j, h].reshape(ORDER, 512) for h in (0, 1)], axis=1)
        rhs = jnp.concatenate(
            [jnp.concatenate([root[j * 4 + k] for k in range(4)], axis=1) for root in (rnext, rown)], axis=0
        )
        half[...] = lax.dot_general(lhs, rhs, NT, preferred_element_type=F32).astype(BF16)
        lhs = jnp.concatenate(
            [roots[j * 16 + k * 4 : j * 16 + k * 4 + 4].reshape(ORDER, SHARE) for k in range(4)], axis=1
        )
        value = jnp.dot(lhs, half[...], preferred_element_type=F32)
        for n, out in enumerate((give, mine)):
            for h in (0, 1):
                at = n * SHARE + h * 128
                out[j, h] = value[:, at : at + 128].astype(BF16).reshape(4, 4, 2, ROWS, 128)
        part = jnp.sum(value * value, axis=0, keepdims=True)
        sham[pl.ds(f * 3 + j, 1), :] = part[:, :128] + part[:, 128:256] + part[:, 256:384] + part[:, 384:]

    def send_part(j):
        for d in (1, 3, 2):
            xx, zz = (x + d) % 4, (z + d) % 4
            for src, yy in ((give, up), (mine, y)):
                remote(
                    src.at[j, 0, :, xx], relayed.at[0, j, 4 - d], sem_s1s.at[j], sem_s1.at[0, j], device(z, xx, c), yy
                ).start()
                remote(
                    src.at[j, 1, zz], relayed.at[1, j, 4 - d], sem_s1s.at[j], sem_s1.at[1, j], device(zz, x, c), yy
                ).start()
        for d in (1, 3, 2, 0):
            xx, zz = (x + d) % 4, (z + d) % 4
            for cc in (0, 1):
                remote(
                    give.at[j, 0, zz, x, cc], got.at[0, j, z, 0, c], sem_hs.at[j], sem_s, device(zz, x, cc), up
                ).start()
                remote(
                    give.at[j, 1, z, xx, cc], got.at[1, j, x, 0, c], sem_hs.at[j], sem_s, device(z, xx, cc), up
                ).start()
                move(mine.at[j, 0, zz, x, cc], got.at[0, j, z, 0, c], sem_os.at[j], sem_s, device(zz, x, cc))
                move(mine.at[j, 1, z, xx, cc], got.at[1, j, x, 0, c], sem_os.at[j], sem_s, device(z, xx, cc))

    def relay_part(j):
        others = pl.ds(1, 3)
        wait_units(3, sem_s1.at[0, j])
        for d in (1, 3, 2, 0):
            zz = (z + d) % 4
            for cc in (0, 1):
                move(
                    relayed.at[0, j, others, zz, cc], got.at[0, j, z, others, c], sem_ss.at[j], sem_s,
                    device(zz, x, cc),
                )
        wait_units(3, sem_s1.at[1, j])
        for d in (1, 3, 2, 0):
            xx = (x + d) % 4
            for cc in (0, 1):
                move(
                    relayed.at[1, j, others, xx, cc], got.at[1, j, x, others, c], sem_ss.at[j], sem_s,
                    device(z, xx, cc),
                )

    def left_rows(j, r):
        value = lax.dot_general(rows_at(j, 0, r), whole[j, 0].reshape(ORDER, 512), NT, preferred_element_type=F32)
        value += lax.dot_general(rows_at(j, 1, r), whole[j, 1].reshape(ORDER, 512), NT, preferred_element_type=F32)
        return value

    def right_rows(j, r):
        at = pl.ds(pl.multiple_of((r % 2) * SHARE, SHARE), SHARE)
        lhs = whole[j, r // 2, :, :, :, :, at].reshape(ORDER, SHARE).T
        return [jnp.dot(lhs, whole[j, h].reshape(ORDER, 512), preferred_element_type=F32) for h in (0, 1)]

    def next_left(j):
        stat_out[j, 0] = left_rows(j, up).astype(BF16)
        remote(stat_out.at[j, 0], stat_in.at[j, 0], sem_ps.at[j], sem_p.at[j], f, up).start()

    def next_right(j):
        for h, value in enumerate(right_rows(j, down)):
            stat_out[j, 1, :, h * 512 : (h + 1) * 512] = value.astype(BF16)
        remote(stat_out.at[j, 1], stat_in.at[j, 1], sem_qs.at[j], sem_q.at[j], f, down).start()

    def own_left(j):
        lstat[j] = 0.9 * lstat[j] + 0.1 * left_rows(j, y)

    def own_right(j):
        for h, value in enumerate(right_rows(j, y)):
            at = slice(h * 512, (h + 1) * 512)
            rstat[j, :, at] = 0.9 * rstat[j, :, at] + 0.1 * value

    def receive_left(j):
        wait_units(8, sem_p.at[j])
        lstat[j] = 0.9 * lstat[j] + 0.1 * stat_in[j, 0].astype(F32)

    def receive_right(j):
        wait_units(8, sem_q.at[j])
        rstat[j] = 0.9 * rstat[j] + 0.1 * stat_in[j, 1].astype(F32)

    stages = [x_line, z_line, y_line]

    def stage_copies(s):
        return [
            remote(tile.at[s], tiles_in.at[s, n], sem_ts.at[s, n], sem_t.at[s, n], *peer)
            for n, peer in enumerate(stages[s])
        ]

    def start_stage(s):
        for copy in stage_copies(s):
            copy.start()

    def end_stage(s):
        for copy in stage_copies(s):
            copy.wait()
        total = tile[s]
        for n in range(len(stages[s])):
            total += tiles_in[s, n]
        tile[s + 1] = total

    def start_sums():
        tile[0] = jnp.zeros((8, 128), F32)
        tile[0, 0:1, :] = jnp.sum(adam[...].T, axis=0, keepdims=True)
        tile[0, 1:2, :] = jnp.sum(sham[...].T, axis=0, keepdims=True)
        start_stage(0)

    def wait_sent(handled):
        for j in range(3):
            wait_units(12, sem_g1s.at[j])
            wait_bytes(blocks.at[pl.ds(0, 21), pl.ds(0, 16), pl.ds(0, 512)], sem_ss.at[j])
            if j in handled:
                wait_units(12, sem_s1s.at[j])
                wait_units(2, sem_hs.at[j])
                wait_bytes(blocks.at[pl.ds(0, 7), pl.ds(0, 16), pl.ds(0, 512)], sem_os.at[j])
                wait_units(12, sem_gs.at[j])
                wait_units(2, sem_ls.at[j])
                wait_units(8, sem_ps.at[j])
                wait_units(8, sem_qs.at[j])
            else:
                wait_units(16, sem_gs.at[j])
                wait_units(6, sem_rs.at[j])
                wait_units(10, sem_ls.at[j])

    load_blocks.wait()
    send_grad(0)
    wait_units(24, sem_in.at[1])
    wait_units(24, sem_in.at[2])

    @pl.when((y + c) % 2 == 0)
    def _():
        send_roots(0, True)
        send_roots(1, False)
        send_roots(2, True)

    @pl.when((y + c) % 2 == 1)
    def _():
        send_roots(0, False)
        send_roots(1, True)

    load_cols.wait()
    load_sec.wait()
    adam[...] = jnp.zeros_like(adam)
    sham[...] = jnp.zeros_like(sham)

    def adam_block(b, carry):
        wide = cols[b].astype(F32)
        new = 0.95 * sec[b] + 0.05 * wide * wide
        sec[b] = new
        value = wide / (jnp.sqrt(new) + 1e-08)
        part = jnp.sum(value * value, axis=0, keepdims=True)
        adam[pl.ds(b, 1), :] = part[:, :128] + part[:, 128:]
        return carry

    lax.fori_loop(0, 64, adam_block, 0)
    load_left.wait()
    load_right.wait()
    relay_grad(0)

    @pl.when((y + c) % 2 == 0)
    def _():
        send_grad(1)
        fill(0)
        relay_grad(1)
        send_grad(2)
        direct(0)
        next_left(0)
        next_right(0)
        own_left(0)
        own_right(0)
        fill(2)
        relay_grad(2)
        send_part(0)
        direct(2)
        send_part(2)
        start_sums()
        relay_part(0)
        next_right(2)
        next_left(2)
        relay_part(1)
        end_stage(0)
        start_stage(1)
        own_left(2)
        own_right(2)
        end_stage(1)
        start_stage(2)
        receive_left(1)
        receive_right(1)
        relay_part(2)
        end_stage(2)
        wait_sent((0, 2))

    @pl.when((y + c) % 2 == 1)
    def _():
        send_grad(1)
        send_roots(2, False)
        fill(1)
        relay_grad(1)
        send_grad(2)
        relay_grad(2)
        direct(1)
        send_part(1)
        next_left(1)
        next_right(1)
        start_sums()
        relay_part(0)
        own_left(1)
        own_right(1)
        relay_part(1)
        end_stage(0)
        start_stage(1)
        receive_left(0)
        receive_right(0)
        end_stage(1)
        start_stage(2)
        relay_part(2)
        receive_left(2)
        receive_right(2)
        end_stage(2)
        wait_sent((1,))

    sums_out[...] = tile[3]
    wait_units(24, sem_s)


def finish_kernel(slots, lstat, rstat, sec, got, sums, left_out, right_out, second_out, out, wide, rows, sem):
    stores = []
    for n, (src, dst) in enumerate(((lstat, left_out), (rstat, right_out), (sec, second_out))):
        copy = pltpu.make_async_copy(src, dst, sem.at[n])
        copy.start()
        stores.append(copy)

    f = lax.axis_index("fsdp")
    x, z = (f // 2) % 4, f // 8
    for n in (0, 1):
        rows[n] = jnp.broadcast_to(sums[n : n + 1, :], (128, 128)).T

    def one(b, carry):
        slot = slots[b]
        j, owner = slot % 3, slot // 3
        c, xs, zs = owner % 2, (owner // 2) % 4, owner // 8
        adam_sq = rows[0, pl.ds(b, 1), :] * (1.0 / 1048576.0)
        sham_sq = rows[1, pl.ds(slot, 1), :] * (1.0 / 1048576.0)
        factor = jnp.sqrt(adam_sq / (sham_sq + 1e-06))
        wide[b, :, :128] = got[0, j, zs, (xs + 4 - x) % 4, c].astype(F32) * factor
        wide[b, :, 128:] = got[1, j, xs, (zs + 4 - z) % 4, c].astype(F32) * factor
        return carry

    for n in range(4):
        part = pl.ds(n * 16, 16)
        lax.fori_loop(n * 16, n * 16 + 16, one, 0)
        copy = pltpu.make_async_copy(wide.at[part], out.at[part], sem.at[3 + n])
        copy.start()
        stores.append(copy)
    for copy in stores:
        copy.wait()


def per_device(grad, second, left, right, left_root, right_root, slot_of_block):
    any_space, vmem = pl.BlockSpec(memory_space=pl.ANY), pl.BlockSpec(memory_space=pltpu.VMEM)
    smem = pl.BlockSpec(memory_space=pltpu.SMEM)
    slots = jnp.arange(96, dtype=jnp.int32)
    named = slot_of_block[None, :] == slots[:, None]
    table = jnp.min(jnp.where(named, jnp.arange(64, dtype=jnp.int32)[None, :], 64), axis=1)
    dma = pltpu.SemaphoreType.DMA
    lstat, rstat, sec, got, sums = pl.pallas_call(
        exchange_kernel,
        name="exchange",
        out_shape=(
            pltpu.VMEM((3, 256, 1024), F32),
            pltpu.VMEM((3, 256, 1024), F32),
            pltpu.VMEM((64, 32, 256), F32),
            pltpu.VMEM((2, 3, 4, 4, 2, 32, 128), BF16),
            pltpu.VMEM((8, 128), F32),
        ),
        in_specs=[smem] + [any_space] * 6,
        out_specs=(vmem,) * 5,
        scratch_shapes=[
            pltpu.VMEM((65, 32, 1024), BF16),
            pltpu.VMEM((64, 32, 256), BF16),
            pltpu.VMEM((2, 3, 4, 4, 32, 512), BF16),
            pltpu.VMEM((2, 3, 4, 4, 32, 512), BF16),
            pltpu.VMEM((3, 2, 4, 4, 2, 32, 512), BF16),
            pltpu.VMEM((48, 256, 256), BF16),
            pltpu.VMEM((12, 256, 256), BF16),
            pltpu.VMEM((12, 256, 256), BF16),
            pltpu.VMEM((1024, 512), BF16),
            pltpu.VMEM((3, 2, 4, 4, 2, 32, 128), BF16),
            pltpu.VMEM((3, 2, 4, 4, 2, 32, 128), BF16),
            pltpu.VMEM((2, 3, 4, 4, 2, 32, 128), BF16),
            pltpu.VMEM((3, 2, 256, 1024), BF16),
            pltpu.VMEM((3, 2, 256, 1024), BF16),
            pltpu.VMEM((128, 128), F32),
            pltpu.VMEM((128, 128), F32),
            pltpu.VMEM((4, 8, 128), F32),
            pltpu.VMEM((3, 7, 8, 128), F32),
            dma((7,)),
            dma((2, 3, 4)), dma((3,)),
            dma((3,)), dma((3,)),
            dma((3,)), dma((3,)),
            dma((3,)), dma((3,)),
            dma((3,)), dma((3,)),
            dma((2, 3)), dma((3,)),
            dma, dma((3,)),
            dma((3,)), dma((3,)),
            dma((3,)), dma((3,)),
            dma((3, 7)), dma((3, 7)),
        ],
        compiler_params=pltpu.CompilerParams(
            collective_id=0, has_side_effects=True, vmem_limit_bytes=EXCHANGE_VMEM
        ),
    )(table, grad, second, left, right, left_root, right_root)
    return pl.pallas_call(
        finish_kernel,
        name="finish",
        out_shape=(
            jax.ShapeDtypeStruct((3, 256, 1024), F32),
            jax.ShapeDtypeStruct((3, 256, 1024), F32),
            jax.ShapeDtypeStruct((64, 32, 256), F32),
            jax.ShapeDtypeStruct((64, 32, 256), F32),
        ),
        in_specs=[smem] + [vmem] * 5,
        out_specs=(any_space,) * 4,
        scratch_shapes=[pltpu.VMEM((64, 32, 256), F32), pltpu.VMEM((2, 128, 128), F32), dma((7,))],
        compiler_params=pltpu.CompilerParams(vmem_limit_bytes=FINISH_VMEM),
    )(slot_of_block, lstat, rstat, sec, got, sums)


def solution(mesh):
    return jax.shard_map(
        per_device,
        mesh=mesh,
        in_specs=(
            P(None, "fsdp", None),
            P(None, "fsdp", "grp"),
            P("fsdp", "grp", None),
            P("fsdp", "grp", None),
            P("fsdp", "grp", None),
            P("fsdp", "grp", None),
            P(),
        ),
        out_specs=(
            P("fsdp", "grp", None),
            P("fsdp", "grp", None),
            P(None, "fsdp", "grp"),
            P(None, "fsdp", "grp"),
        ),
        check_vma=False,
    )
```

```python
import jax
import jax.numpy as jnp
from jax import lax
from jax.experimental import pallas as pl
from jax.experimental.pallas import tpu as pltpu
from jax.sharding import PartitionSpec as P

MESH = pl.DeviceIdType.MESH
F32, BF16 = jnp.float32, jnp.bfloat16
NT = (((1,), (1,)), ((), ()))
EXCHANGE_VMEM = 50 * 2**20
FINISH_VMEM = 16 * 2**20
SHARE, ROWS, ORDER = 256, 32, 1024


def exchange_kernel(
    slots, grad, second, left, right, left_root, right_root,
    lstat, rstat, sec, got, sums_out,
    table, ranks, blocks, cols, packed, passing, whole, roots, rown, rnext, half,
    mine, give, relayed, stat_out, stat_in, adam, sham, tile, tiles_in,
    sem_in, sem_g1, sem_g1s, sem_g, sem_gs, sem_l, sem_ls, sem_r, sem_rs,
    sem_os, sem_hs, sem_s1, sem_s1s, sem_s, sem_ss, sem_p, sem_ps, sem_q, sem_qs, sem_t, sem_ts,
):
    f, y = lax.axis_index("fsdp"), lax.axis_index("grp")
    c, x, z = f % 2, (f // 2) % 4, f // 8
    up, down, across = (y + 1 + 2 * c) % 4, (y + 3 + 2 * c) % 4, (y + 2) % 4

    def device(zz, xx, cc):
        return zz * 8 + xx * 2 + cc


    def remote(src, dst, send, recv, ff, yy):
        return pltpu.make_async_remote_copy(
            src_ref=src, dst_ref=dst, send_sem=send, recv_sem=recv, device_id=(ff, yy), device_id_type=MESH
        )

    def move(src, dst, send, recv, ff):
        @pl.when(ff == f)
        def _():
            pltpu.make_async_copy(src, dst, recv).start()

        @pl.when(ff != f)
        def _():
            remote(src, dst, send, recv, ff, y).start()

    def wait_bytes(ref, sem):
        pltpu.make_async_copy(ref, ref, sem).wait()

    def wait_units(n, sem):
        wait_bytes(blocks.at[pl.ds(0, n)], sem)

    x_line = [(device(z, (x + d) % 4, c), y) for d in (1, 2, 3)]
    x_line += [(device(z, (x + d) % 4, 1 - c), y) for d in (0, 1, 2, 3)]
    z_line = [(device((z + d) % 4, x, c), y) for d in (1, 2, 3)]
    z_other = [(device((z + d) % 4, x, 1 - c), y) for d in (1, 2, 3)]
    y_line = [(f, (y + d) % 4) for d in (1, 2, 3)]
    senders = x_line + z_line + z_other + y_line
    for cc, yy in ((0, (y + 3) % 4), (1, (y + 1) % 4)):
        senders += [(device(z, (x + d) % 4, cc), yy) for d in (0, 1, 2, 3)]
        senders += [(device((z + d) % 4, x, cc), yy) for d in (1, 2, 3)]
    barrier = pltpu.get_barrier_semaphore()
    for peer in senders:
        pl.semaphore_signal(barrier, inc=1, device_id=peer, device_id_type=MESH)

    lane = lax.broadcasted_iota(jnp.int32, (8, 128), 1)
    rank = jnp.full((8, 128), 64, jnp.int32)
    for b in range(64):
        rank = jnp.where(lane == slots[b], b, rank)
    ranks[...] = rank

    def load(src, dst, n):
        copy = pltpu.make_async_copy(src, dst, sem_in.at[n])
        copy.start()
        return copy

    load_blocks = load(grad, blocks.at[pl.ds(0, 64)], 0)
    for j in range(3):
        for k in range(4):
            load(left_root.at[j, :, pl.ds(k * SHARE, SHARE)], roots.at[j * 16 + k * 4 + y], 1)
            load(right_root.at[j, :, pl.ds(k * SHARE, SHARE)], rown.at[j * 4 + k], 2)
    load_table = load(ranks, table, 7)
    load_cols = load(grad.at[:, :, pl.ds(pl.multiple_of(y * SHARE, SHARE), SHARE)], cols, 3)
    load_sec = load(second, sec, 4)
    load_left = load(left, lstat, 5)
    load_right = load(right, rstat, 6)

    blocks[64] = jnp.zeros((ROWS, ORDER), BF16)


    def to_handler(j, route, piece, zs, xs, other):
        cc = (y + j) % 2
        ff = device(other, x, cc) if route == 0 else device(z, other, cc)
        move(piece, whole.at[j, route, zs, xs, c], sem_gs.at[j], sem_g.at[j], ff)

    def pack_grad(j):
        cc = (y + j) % 2

        def pack(n, carry):
            zz, xx = n // 4, n % 4
            piece = blocks[table[0, device(zz, xx, cc) * 3 + j]]
            packed[0, j, xx, zz] = piece[:, :512]
            packed[1, j, zz, xx] = piece[:, 512:]
            return carry

        lax.fori_loop(0, 16, pack, 0)

    def send_lines(j):
        for d in (1, 3, 2):
            xx, zz = (x + d) % 4, (z + d) % 4
            remote(
                packed.at[0, j, xx], passing.at[0, j, x], sem_g1s.at[j], sem_g1.at[0, j, x], device(z, xx, c), y
            ).start()
            remote(
                packed.at[1, j, zz], passing.at[1, j, z], sem_g1s.at[j], sem_g1.at[1, j, z], device(zz, x, c), y
            ).start()

    def send_own(j):
        for d in (1, 3, 2, 0):
            xx, zz = (x + d) % 4, (z + d) % 4
            to_handler(j, 0, packed.at[0, j, x, zz], z, x, zz)
            to_handler(j, 1, packed.at[1, j, z, xx], z, x, xx)

    def relay_grad(j):
        for e in (1, 3, 2):
            xs, zs = (x + e) % 4, (z + e) % 4
            wait_units(2, sem_g1.at[0, j, xs])
            for d in (1, 3, 2, 0):
                to_handler(j, 0, passing.at[0, j, xs, (z + d) % 4], z, xs, (z + d) % 4)
            wait_units(2, sem_g1.at[1, j, zs])
            for d in (1, 3, 2, 0):
                to_handler(j, 1, passing.at[1, j, zs, (x + d) % 4], zs, x, (x + d) % 4)

    def send_roots(j, handled):
        def block(k, yy):
            at = roots.at[j * 16 + k * 4 + y]
            remote(at, at, sem_ls.at[j], sem_l.at[j], f, yy).start()

        if handled:
            block(y, across)
        else:
            for k in (y, up, across):
                block(k, down)
                at = j * 4 + k
                remote(rown.at[at], rnext.at[at], sem_rs.at[j], sem_r.at[j], f, down).start()
            for k in (y, down):
                block(k, up)

    def fill(j):
        wait_units(12, sem_l.at[j])
        for r, k in ((up, y), (across, y), (down, y), (across, up), (down, up), (across, down)):
            roots[j * 16 + k * 4 + r] = roots[j * 16 + r * 4 + k].T
        rnext[j * 4 + y] = rown[j * 4 + up].T

    def rows_at(j, h, r):
        return whole[j, h, r].reshape(SHARE, 512)

    def direct(j):
        wait_units(6, sem_r.at[j])
        wait_units(32, sem_g.at[j])
        lhs = jnp.concatenate([whole[j, h].reshape(ORDER, 512) for h in (0, 1)], axis=1)
        rhs = jnp.concatenate(
            [jnp.concatenate([root[j * 4 + k] for k in range(4)], axis=1) for root in (rnext, rown)], axis=0
        )
        half[...] = lax.dot_general(lhs, rhs, NT, preferred_element_type=F32).astype(BF16)
        lhs = jnp.concatenate(
            [roots[j * 16 + k * 4 : j * 16 + k * 4 + 4].reshape(ORDER, SHARE) for k in range(4)], axis=1
        )
        value = jnp.dot(lhs, half[...], preferred_element_type=F32)
        for n, out in enumerate((give, mine)):
            for h in (0, 1):
                at = n * SHARE + h * 128
                out[j, h] = value[:, at : at + 128].astype(BF16).reshape(4, 4, 2, ROWS, 128)
        part = jnp.sum(value * value, axis=0, keepdims=True)
        sham[pl.ds(f * 3 + j, 1), :] = part[:, :128] + part[:, 128:256] + part[:, 256:384] + part[:, 384:]

    def direct_first(j):
        wait_units(6, sem_r.at[j])
        wait_units(32, sem_g.at[j])
        direct_one(j, rnext, 0, give)

    def direct_one(j, root, n, out):
        at = slice(n * SHARE, (n + 1) * SHARE)
        lhs = jnp.concatenate([whole[j, h].reshape(ORDER, 512) for h in (0, 1)], axis=1)
        rhs = jnp.concatenate([root[j * 4 + k] for k in range(4)], axis=1)
        half[:, at] = lax.dot_general(lhs, rhs, NT, preferred_element_type=F32).astype(BF16)
        lhs = jnp.concatenate(
            [roots[j * 16 + k * 4 : j * 16 + k * 4 + 4].reshape(ORDER, SHARE) for k in range(4)], axis=1
        )
        value = jnp.dot(lhs, half[:, at], preferred_element_type=F32)
        for h in (0, 1):
            out[j, h] = value[:, h * 128 : (h + 1) * 128].astype(BF16).reshape(4, 4, 2, ROWS, 128)
        part = jnp.sum(value * value, axis=0, keepdims=True)
        sham[pl.ds(f * 3 + j, 1), :] += part[:, :128] + part[:, 128:]

    def direct_second(j):
        direct_one(j, rown, 1, mine)

    def send_give(j):
        for d in (1, 3, 2):
            xx, zz = (x + d) % 4, (z + d) % 4
            remote(
                give.at[j, 0, :, xx], relayed.at[0, j, 4 - d], sem_s1s.at[j], sem_s1.at[0, j], device(z, xx, c), up
            ).start()
            remote(
                give.at[j, 1, zz], relayed.at[1, j, 4 - d], sem_s1s.at[j], sem_s1.at[1, j], device(zz, x, c), up
            ).start()
        for d in (1, 3, 2, 0):
            xx, zz = (x + d) % 4, (z + d) % 4
            for cc in (0, 1):
                remote(
                    give.at[j, 0, zz, x, cc], got.at[0, j, z, 0, c], sem_hs.at[j], sem_s, device(zz, x, cc), up
                ).start()
                remote(
                    give.at[j, 1, z, xx, cc], got.at[1, j, x, 0, c], sem_hs.at[j], sem_s, device(z, xx, cc), up
                ).start()

    def send_mine(j):
        for d in (1, 3, 2):
            xx, zz = (x + d) % 4, (z + d) % 4
            remote(
                mine.at[j, 0, :, xx], relayed.at[0, j, 4 - d], sem_s1s.at[j], sem_s1.at[0, j], device(z, xx, c), y
            ).start()
            remote(
                mine.at[j, 1, zz], relayed.at[1, j, 4 - d], sem_s1s.at[j], sem_s1.at[1, j], device(zz, x, c), y
            ).start()
        for d in (1, 3, 2, 0):
            xx, zz = (x + d) % 4, (z + d) % 4
            for cc in (0, 1):
                move(mine.at[j, 0, zz, x, cc], got.at[0, j, z, 0, c], sem_os.at[j], sem_s, device(zz, x, cc))
                move(mine.at[j, 1, z, xx, cc], got.at[1, j, x, 0, c], sem_os.at[j], sem_s, device(z, xx, cc))

    def relay_part(j):
        others = pl.ds(1, 3)
        wait_units(3, sem_s1.at[0, j])
        for d in (1, 3, 2, 0):
            zz = (z + d) % 4
            for cc in (0, 1):
                move(
                    relayed.at[0, j, others, zz, cc], got.at[0, j, z, others, c], sem_ss.at[j], sem_s,
                    device(zz, x, cc),
                )
        wait_units(3, sem_s1.at[1, j])
        for d in (1, 3, 2, 0):
            xx = (x + d) % 4
            for cc in (0, 1):
                move(
                    relayed.at[1, j, others, xx, cc], got.at[1, j, x, others, c], sem_ss.at[j], sem_s,
                    device(z, xx, cc),
                )

    def left_part(j, r, h):
        value = lax.dot_general(
            rows_at(j, 0, r), whole[j, 0, 2 * h : 2 * h + 2].reshape(512, 512), NT, preferred_element_type=F32
        )
        value += lax.dot_general(
            rows_at(j, 1, r), whole[j, 1, 2 * h : 2 * h + 2].reshape(512, 512), NT, preferred_element_type=F32
        )
        return value

    def right_parts(j, r):
        at = pl.ds(pl.multiple_of((r % 2) * SHARE, SHARE), SHARE)
        lhs = whole[j, r // 2, :, :, :, :, at].reshape(ORDER, SHARE).T
        return [jnp.dot(lhs, whole[j, h].reshape(ORDER, 512), preferred_element_type=F32) for h in (0, 1)]

    def left_up(j):
        stat_out[j, 0] = left_part(j, up, 0).astype(BF16)
        remote(stat_out.at[j, 0], stat_in.at[j, 0], sem_ps.at[j], sem_p.at[j], f, up).start()

    def left_down(j):
        stat_out[j, 1] = left_part(j, down, 1).astype(BF16)
        remote(stat_out.at[j, 1], stat_in.at[j, 1], sem_qs.at[j], sem_q.at[j], f, down).start()

    def next_right(j):
        both = pl.ds(2, 2)
        for h, value in enumerate(right_parts(j, down)):
            stat_out[j, 2 + h] = value.astype(BF16)
        remote(stat_out.at[j, both], stat_in.at[j, both], sem_qs.at[j], sem_q.at[j], f, down).start()

    def own_left(j):
        for h in (0, 1):
            at = slice(h * 512, (h + 1) * 512)
            lstat[j, :, at] = 0.9 * lstat[j, :, at] + 0.1 * left_part(j, y, h)

    def own_right(j):
        for h, value in enumerate(right_parts(j, y)):
            at = slice(h * 512, (h + 1) * 512)
            rstat[j, :, at] = 0.9 * rstat[j, :, at] + 0.1 * value

    def receive_up(j):
        wait_units(4, sem_p.at[j])
        lstat[j, :, :512] = 0.9 * lstat[j, :, :512] + 0.1 * stat_in[j, 0].astype(F32)

    def receive_down(j):
        wait_units(12, sem_q.at[j])
        lstat[j, :, 512:] = 0.9 * lstat[j, :, 512:] + 0.1 * stat_in[j, 1].astype(F32)
        rstat[j, :, :512] = 0.9 * rstat[j, :, :512] + 0.1 * stat_in[j, 2].astype(F32)
        rstat[j, :, 512:] = 0.9 * rstat[j, :, 512:] + 0.1 * stat_in[j, 3].astype(F32)

    stages = [x_line, z_line, y_line]

    def stage_copies(s):
        return [
            remote(tile.at[s], tiles_in.at[s, n], sem_ts.at[s, n], sem_t.at[s, n], *peer)
            for n, peer in enumerate(stages[s])
        ]

    def start_stage(s):
        for copy in stage_copies(s):
            copy.start()

    def end_stage(s):
        for copy in stage_copies(s):
            copy.wait()
        total = tile[s]
        for n in range(len(stages[s])):
            total += tiles_in[s, n]
        tile[s + 1] = total

    def start_sums():
        tile[0] = jnp.zeros((8, 128), F32)
        tile[0, 0:1, :] = jnp.sum(adam[...].T, axis=0, keepdims=True)
        tile[0, 1:2, :] = jnp.sum(sham[...].T, axis=0, keepdims=True)
        start_stage(0)

    def wait_sent(handled):
        for j in range(3):
            wait_units(12, sem_g1s.at[j])
            wait_bytes(blocks.at[pl.ds(0, 21), pl.ds(0, 16), pl.ds(0, 512)], sem_ss.at[j])
            if j in handled:
                wait_units(12, sem_s1s.at[j])
                wait_units(2, sem_hs.at[j])
                wait_bytes(blocks.at[pl.ds(0, 7), pl.ds(0, 16), pl.ds(0, 512)], sem_os.at[j])
                wait_units(12, sem_gs.at[j])
                wait_units(2, sem_ls.at[j])
                wait_units(4, sem_ps.at[j])
                wait_units(12, sem_qs.at[j])
            else:
                wait_units(16, sem_gs.at[j])
                wait_units(6, sem_rs.at[j])
                wait_units(10, sem_ls.at[j])

    load_blocks.wait()
    load_table.wait()
    pack_grad(0)
    pl.semaphore_wait(barrier, 30)
    send_lines(0)
    send_own(0)
    wait_units(24, sem_in.at[1])
    wait_units(24, sem_in.at[2])

    @pl.when((y + c) % 2 == 0)
    def _():
        send_roots(0, True)
        send_roots(1, False)
        send_roots(2, True)

    @pl.when((y + c) % 2 == 1)
    def _():
        send_roots(0, False)
        send_roots(1, True)

    load_cols.wait()
    load_sec.wait()
    adam[...] = jnp.zeros_like(adam)
    sham[...] = jnp.zeros_like(sham)

    def adam_block(b, carry):
        wide = cols[b].astype(F32)
        new = 0.95 * sec[b] + 0.05 * wide * wide
        sec[b] = new
        value = wide / (jnp.sqrt(new) + 1e-08)
        part = jnp.sum(value * value, axis=0, keepdims=True)
        adam[pl.ds(b, 1), :] = part[:, :128] + part[:, 128:]
        return carry

    lax.fori_loop(0, 64, adam_block, 0)
    load_left.wait()
    load_right.wait()
    pack_grad(1)
    pack_grad(2)
    relay_grad(0)

    @pl.when((y + c) % 2 == 0)
    def _():
        send_lines(1)
        send_own(1)
        fill(0)
        relay_grad(1)
        send_lines(2)
        send_own(2)
        direct(0)
        send_give(0)
        left_up(0)
        left_down(0)
        next_right(0)
        own_left(0)
        own_right(0)
        fill(2)
        relay_grad(2)
        send_mine(0)
        relay_part(0)
        direct(2)
        start_sums()
        send_give(2)
        send_mine(2)
        next_right(2)
        left_down(2)
        relay_part(1)
        end_stage(0)
        start_stage(1)
        own_left(2)
        own_right(2)
        left_up(2)
        relay_part(2)
        end_stage(1)
        start_stage(2)
        receive_up(1)
        receive_down(1)
        end_stage(2)
        wait_sent((0, 2))

    @pl.when((y + c) % 2 == 1)
    def _():
        send_lines(1)
        send_own(1)
        send_roots(2, False)
        fill(1)
        relay_grad(1)
        send_lines(2)
        send_own(2)
        relay_grad(2)
        direct(1)
        start_sums()
        send_give(1)
        send_mine(1)
        left_up(1)
        left_down(1)
        next_right(1)
        relay_part(0)
        own_left(1)
        own_right(1)
        relay_part(1)
        end_stage(0)
        start_stage(1)
        receive_up(0)
        receive_down(0)
        relay_part(2)
        end_stage(1)
        start_stage(2)
        receive_down(2)
        receive_up(2)
        end_stage(2)
        wait_sent((1,))

    sums_out[...] = tile[3]
    wait_units(24, sem_s)


def finish_kernel(slots, lstat, rstat, sec, got, sums, left_out, right_out, second_out, out, wide, rows, sem):
    stores = []
    for n, (src, dst) in enumerate(((lstat, left_out), (rstat, right_out), (sec, second_out))):
        copy = pltpu.make_async_copy(src, dst, sem.at[n])
        copy.start()
        stores.append(copy)

    f = lax.axis_index("fsdp")
    x, z = (f // 2) % 4, f // 8
    for n in (0, 1):
        rows[n] = jnp.broadcast_to(sums[n : n + 1, :], (128, 128)).T

    def one(b, carry):
        slot = slots[b]
        j, owner = slot % 3, slot // 3
        c, xs, zs = owner % 2, (owner // 2) % 4, owner // 8
        adam_sq = rows[0, pl.ds(b, 1), :] * (1.0 / 1048576.0)
        sham_sq = rows[1, pl.ds(slot, 1), :] * (1.0 / 1048576.0)
        factor = jnp.sqrt(adam_sq / (sham_sq + 1e-06))
        wide[b, :, :128] = got[0, j, zs, (xs + 4 - x) % 4, c].astype(F32) * factor
        wide[b, :, 128:] = got[1, j, xs, (zs + 4 - z) % 4, c].astype(F32) * factor
        return carry

    for n in range(4):
        part = pl.ds(n * 16, 16)
        lax.fori_loop(n * 16, n * 16 + 16, one, 0)
        copy = pltpu.make_async_copy(wide.at[part], out.at[part], sem.at[3 + n])
        copy.start()
        stores.append(copy)
    for copy in stores:
        copy.wait()


def per_device(grad, second, left, right, left_root, right_root, slot_of_block):
    any_space, vmem = pl.BlockSpec(memory_space=pl.ANY), pl.BlockSpec(memory_space=pltpu.VMEM)
    smem = pl.BlockSpec(memory_space=pltpu.SMEM)
    dma = pltpu.SemaphoreType.DMA
    lstat, rstat, sec, got, sums = pl.pallas_call(
        exchange_kernel,
        name="exchange",
        out_shape=(
            pltpu.VMEM((3, 256, 1024), F32),
            pltpu.VMEM((3, 256, 1024), F32),
            pltpu.VMEM((64, 32, 256), F32),
            pltpu.VMEM((2, 3, 4, 4, 2, 32, 128), BF16),
            pltpu.VMEM((8, 128), F32),
        ),
        in_specs=[smem] + [any_space] * 6,
        out_specs=(vmem,) * 5,
        scratch_shapes=[
            pltpu.SMEM((8, 128), jnp.int32),
            pltpu.VMEM((8, 128), jnp.int32),
            pltpu.VMEM((65, 32, 1024), BF16),
            pltpu.VMEM((64, 32, 256), BF16),
            pltpu.VMEM((2, 3, 4, 4, 32, 512), BF16),
            pltpu.VMEM((2, 3, 4, 4, 32, 512), BF16),
            pltpu.VMEM((3, 2, 4, 4, 2, 32, 512), BF16),
            pltpu.VMEM((48, 256, 256), BF16),
            pltpu.VMEM((12, 256, 256), BF16),
            pltpu.VMEM((12, 256, 256), BF16),
            pltpu.VMEM((1024, 512), BF16),
            pltpu.VMEM((3, 2, 4, 4, 2, 32, 128), BF16),
            pltpu.VMEM((3, 2, 4, 4, 2, 32, 128), BF16),
            pltpu.VMEM((2, 3, 4, 4, 2, 32, 128), BF16),
            pltpu.VMEM((3, 4, 256, 512), BF16),
            pltpu.VMEM((3, 4, 256, 512), BF16),
            pltpu.VMEM((128, 128), F32),
            pltpu.VMEM((128, 128), F32),
            pltpu.VMEM((4, 8, 128), F32),
            pltpu.VMEM((3, 7, 8, 128), F32),
            dma((8,)),
            dma((2, 3, 4)), dma((3,)),
            dma((3,)), dma((3,)),
            dma((3,)), dma((3,)),
            dma((3,)), dma((3,)),
            dma((3,)), dma((3,)),
            dma((2, 3)), dma((3,)),
            dma, dma((3,)),
            dma((3,)), dma((3,)),
            dma((3,)), dma((3,)),
            dma((3, 7)), dma((3, 7)),
        ],
        compiler_params=pltpu.CompilerParams(
            collective_id=0, has_side_effects=True, vmem_limit_bytes=EXCHANGE_VMEM
        ),
    )(slot_of_block, grad, second, left, right, left_root, right_root)
    return pl.pallas_call(
        finish_kernel,
        name="finish",
        out_shape=(
            jax.ShapeDtypeStruct((3, 256, 1024), F32),
            jax.ShapeDtypeStruct((3, 256, 1024), F32),
            jax.ShapeDtypeStruct((64, 32, 256), F32),
            jax.ShapeDtypeStruct((64, 32, 256), F32),
        ),
        in_specs=[smem] + [vmem] * 5,
        out_specs=(any_space,) * 4,
        scratch_shapes=[pltpu.VMEM((64, 32, 256), F32), pltpu.VMEM((2, 128, 128), F32), dma((7,))],
        compiler_params=pltpu.CompilerParams(vmem_limit_bytes=FINISH_VMEM),
    )(slot_of_block, lstat, rstat, sec, got, sums)


def solution(mesh):
    return jax.shard_map(
        per_device,
        mesh=mesh,
        in_specs=(
            P(None, "fsdp", None),
            P(None, "fsdp", "grp"),
            P("fsdp", "grp", None),
            P("fsdp", "grp", None),
            P("fsdp", "grp", None),
            P("fsdp", "grp", None),
            P(),
        ),
        out_specs=(
            P("fsdp", "grp", None),
            P("fsdp", "grp", None),
            P(None, "fsdp", "grp"),
            P(None, "fsdp", "grp"),
        ),
        check_vma=False,
    )
```

```python
import jax
import jax.numpy as jnp
from jax import lax
from jax.experimental import pallas as pl
from jax.experimental.pallas import tpu as pltpu
from jax.sharding import PartitionSpec as P

MESH = pl.DeviceIdType.MESH
F32, BF16 = jnp.float32, jnp.bfloat16
NT = (((1,), (1,)), ((), ()))
EXCHANGE_VMEM = 50 * 2**20
FINISH_VMEM = 16 * 2**20
SHARE, ROWS, ORDER = 256, 32, 1024


def exchange_kernel(
    slots, grad, second, left, right, left_root, right_root,
    lstat, rstat, sec, got, sums_out,
    table, ranks, blocks, cols, packed, passing, whole, roots, rown, rnext, half,
    mine, give, relayed, stat_out, stat_in, adam, sham, tile, tiles_in,
    sem_in, sem_g1, sem_g1s, sem_g, sem_gs, sem_l, sem_ls, sem_r, sem_rs,
    sem_s1, sem_s1s, sem_s, sem_ss, sem_p, sem_ps, sem_q, sem_qs, sem_t, sem_ts,
):
    f, y = lax.axis_index("fsdp"), lax.axis_index("grp")
    c, x, z = f % 2, (f // 2) % 4, f // 8
    up, down, across = (y + 1 + 2 * c) % 4, (y + 3 + 2 * c) % 4, (y + 2) % 4

    def device(zz, xx, cc):
        return zz * 8 + xx * 2 + cc


    def remote(src, dst, send, recv, ff, yy):
        return pltpu.make_async_remote_copy(
            src_ref=src, dst_ref=dst, send_sem=send, recv_sem=recv, device_id=(ff, yy), device_id_type=MESH
        )

    def move(src, dst, send, recv, ff):
        @pl.when(ff == f)
        def _():
            pltpu.make_async_copy(src, dst, recv).start()

        @pl.when(ff != f)
        def _():
            remote(src, dst, send, recv, ff, y).start()

    def wait_bytes(ref, sem):
        pltpu.make_async_copy(ref, ref, sem).wait()

    def wait_units(n, sem):
        wait_bytes(blocks.at[pl.ds(0, n)], sem)

    x_line = [(device(z, (x + d) % 4, c), y) for d in (1, 2, 3)]
    x_line += [(device(z, (x + d) % 4, 1 - c), y) for d in (0, 1, 2, 3)]
    z_line = [(device((z + d) % 4, x, c), y) for d in (1, 2, 3)]
    z_other = [(device((z + d) % 4, x, 1 - c), y) for d in (1, 2, 3)]
    y_line = [(f, (y + d) % 4) for d in (1, 2, 3)]
    senders = x_line + z_line + z_other + y_line
    senders += [(device(z, (x + d) % 4, c), down) for d in (1, 2, 3)]
    senders += [(device((z + d) % 4, x, c), down) for d in (1, 2, 3)]
    barrier = pltpu.get_barrier_semaphore()
    for peer in senders:
        pl.semaphore_signal(barrier, inc=1, device_id=peer, device_id_type=MESH)

    lane = lax.broadcasted_iota(jnp.int32, (8, 128), 1)
    rank = jnp.full((8, 128), 64, jnp.int32)
    for b in range(64):
        rank = jnp.where(lane == slots[b], b, rank)
    ranks[...] = rank

    def load(src, dst, n):
        copy = pltpu.make_async_copy(src, dst, sem_in.at[n])
        copy.start()
        return copy

    load_blocks = load(grad, blocks.at[pl.ds(0, 64)], 0)
    for j in range(3):
        for k in range(4):
            load(left_root.at[j, :, pl.ds(k * SHARE, SHARE)], roots.at[j * 16 + k * 4 + y], 1)
            load(right_root.at[j, :, pl.ds(k * SHARE, SHARE)], rown.at[j * 4 + k], 2)
    load_table = load(ranks, table, 7)
    load_cols = load(grad.at[:, :, pl.ds(pl.multiple_of(y * SHARE, SHARE), SHARE)], cols, 3)
    load_sec = load(second, sec, 4)
    load_left = load(left, lstat, 5)
    load_right = load(right, rstat, 6)

    blocks[64] = jnp.zeros((ROWS, ORDER), BF16)


    def to_handler(j, route, piece, zs, xs, other):
        cc = (y + j) % 2
        ff = device(other, x, cc) if route == 0 else device(z, other, cc)
        move(piece, whole.at[j, route, zs, xs, c], sem_gs.at[j], sem_g.at[j], ff)

    def pack_grad(j):
        cc = (y + j) % 2

        def pack(n, carry):
            zz, xx = n // 4, n % 4
            piece = blocks[table[0, device(zz, xx, cc) * 3 + j]]
            packed[0, j, xx, zz] = piece[:, :512]
            packed[1, j, zz, xx] = piece[:, 512:]
            return carry

        lax.fori_loop(0, 16, pack, 0)

    def send_lines(j):
        for d in (1, 3, 2):
            xx, zz = (x + d) % 4, (z + d) % 4
            remote(
                packed.at[0, j, xx], passing.at[0, j, x], sem_g1s.at[j], sem_g1.at[0, j, x], device(z, xx, c), y
            ).start()
            remote(
                packed.at[1, j, zz], passing.at[1, j, z], sem_g1s.at[j], sem_g1.at[1, j, z], device(zz, x, c), y
            ).start()

    def send_own(j):
        for d in (1, 3, 2, 0):
            xx, zz = (x + d) % 4, (z + d) % 4
            to_handler(j, 0, packed.at[0, j, x, zz], z, x, zz)
            to_handler(j, 1, packed.at[1, j, z, xx], z, x, xx)

    def relay_grad(j, distances=(1, 3, 2)):
        for e in distances:
            xs, zs = (x + e) % 4, (z + e) % 4
            wait_units(2, sem_g1.at[0, j, xs])
            for d in (1, 3, 2, 0):
                to_handler(j, 0, passing.at[0, j, xs, (z + d) % 4], z, xs, (z + d) % 4)
            wait_units(2, sem_g1.at[1, j, zs])
            for d in (1, 3, 2, 0):
                to_handler(j, 1, passing.at[1, j, zs, (x + d) % 4], zs, x, (x + d) % 4)

    def send_roots(j, handled):
        def block(k, yy):
            at = roots.at[j * 16 + k * 4 + y]
            remote(at, at, sem_ls.at[j], sem_l.at[j], f, yy).start()

        if handled:
            block(y, across)
        else:
            for k in (y, up, across):
                block(k, down)
                at = j * 4 + k
                remote(rown.at[at], rnext.at[at], sem_rs.at[j], sem_r.at[j], f, down).start()
            for k in (y, down):
                block(k, up)

    def fill(j):
        wait_units(12, sem_l.at[j])
        for r, k in ((up, y), (across, y), (down, y), (across, up), (down, up), (across, down)):
            roots[j * 16 + k * 4 + r] = roots[j * 16 + r * 4 + k].T
        rnext[j * 4 + y] = rown[j * 4 + up].T

    def rows_at(j, h, r):
        return whole[j, h, r].reshape(SHARE, 512)

    def direct(j):
        wait_units(6, sem_r.at[j])
        wait_units(32, sem_g.at[j])
        lhs = jnp.concatenate([whole[j, h].reshape(ORDER, 512) for h in (0, 1)], axis=1)
        rhs = jnp.concatenate(
            [jnp.concatenate([root[j * 4 + k] for k in range(4)], axis=1) for root in (rnext, rown)], axis=0
        )
        half[...] = lax.dot_general(lhs, rhs, NT, preferred_element_type=F32).astype(BF16)
        lhs = jnp.concatenate(
            [roots[j * 16 + k * 4 : j * 16 + k * 4 + 4].reshape(ORDER, SHARE) for k in range(4)], axis=1
        )
        value = jnp.dot(lhs, half[...], preferred_element_type=F32)
        for n, out in enumerate((give, mine)):
            piece = value[:, n * SHARE : (n + 1) * SHARE].astype(BF16).reshape(4, 4, 2, ROWS, SHARE)
            out[j, 0] = piece[:, :, 0]
            out[j, 1] = piece[:, :, 1]
        part = jnp.sum(value * value, axis=0, keepdims=True)
        sham[pl.ds(f * 3 + j, 1), :] = part[:, :128] + part[:, 128:256] + part[:, 256:384] + part[:, 384:]

    def send_give(j):
        for d in (1, 3, 2, 0):
            xx, zz = (x + d) % 4, (z + d) % 4
            e = (4 - d) % 4
            remote(
                give.at[j, 0, :, xx], relayed.at[0, j, e], sem_s1s.at[j], sem_s1.at[0, j], device(z, xx, c), up
            ).start()
            remote(
                give.at[j, 1, zz], relayed.at[1, j, e], sem_s1s.at[j], sem_s1.at[1, j], device(zz, x, c), up
            ).start()

    def send_mine(j):
        for d in (1, 3, 2):
            xx, zz = (x + d) % 4, (z + d) % 4
            remote(
                mine.at[j, 0, :, xx], relayed.at[0, j, 4 - d], sem_s1s.at[j], sem_s1.at[0, j], device(z, xx, c), y
            ).start()
            remote(
                mine.at[j, 1, zz], relayed.at[1, j, 4 - d], sem_s1s.at[j], sem_s1.at[1, j], device(zz, x, c), y
            ).start()
        pltpu.make_async_copy(mine.at[j, 0, :, x], relayed.at[0, j, 0], sem_s1.at[0, j]).start()
        pltpu.make_async_copy(mine.at[j, 1, z], relayed.at[1, j, 0], sem_s1.at[1, j]).start()

    def relay_part(j):
        wait_units(4, sem_s1.at[0, j])
        for d in (1, 3, 2, 0):
            zz = (z + d) % 4
            move(relayed.at[0, j, :, zz], got.at[j, z, :, c], sem_ss.at[j], sem_s, device(zz, x, 0))
        wait_units(4, sem_s1.at[1, j])
        for d in (1, 3, 2, 0):
            xx = (x + d) % 4
            move(relayed.at[1, j, :, xx], got.at[j, x, :, c], sem_ss.at[j], sem_s, device(z, xx, 1))

    def left_part(j, r, h):
        value = lax.dot_general(
            rows_at(j, 0, r), whole[j, 0, 2 * h : 2 * h + 2].reshape(512, 512), NT, preferred_element_type=F32
        )
        value += lax.dot_general(
            rows_at(j, 1, r), whole[j, 1, 2 * h : 2 * h + 2].reshape(512, 512), NT, preferred_element_type=F32
        )
        return value

    def right_parts(j, r):
        at = pl.ds(pl.multiple_of((r % 2) * SHARE, SHARE), SHARE)
        lhs = whole[j, r // 2, :, :, :, :, at].reshape(ORDER, SHARE).T
        return [jnp.dot(lhs, whole[j, h].reshape(ORDER, 512), preferred_element_type=F32) for h in (0, 1)]

    def left_up(j):
        stat_out[j, 0] = left_part(j, up, 0).astype(BF16)
        remote(stat_out.at[j, 0], stat_in.at[j, 0], sem_ps.at[j], sem_p.at[j], f, up).start()

    def left_down(j):
        stat_out[j, 1] = left_part(j, down, 1).astype(BF16)
        remote(stat_out.at[j, 1], stat_in.at[j, 1], sem_qs.at[j], sem_q.at[j], f, down).start()

    def next_right(j):
        both = pl.ds(2, 2)
        for h, value in enumerate(right_parts(j, down)):
            stat_out[j, 2 + h] = value.astype(BF16)
        remote(stat_out.at[j, both], stat_in.at[j, both], sem_qs.at[j], sem_q.at[j], f, down).start()

    def own_left(j):
        for h in (0, 1):
            at = slice(h * 512, (h + 1) * 512)
            lstat[j, :, at] = 0.9 * lstat[j, :, at] + 0.1 * left_part(j, y, h)

    def own_right(j):
        for h, value in enumerate(right_parts(j, y)):
            at = slice(h * 512, (h + 1) * 512)
            rstat[j, :, at] = 0.9 * rstat[j, :, at] + 0.1 * value

    def receive_up(j):
        wait_units(4, sem_p.at[j])
        lstat[j, :, :512] = 0.9 * lstat[j, :, :512] + 0.1 * stat_in[j, 0].astype(F32)

    def receive_down(j):
        wait_units(12, sem_q.at[j])
        lstat[j, :, 512:] = 0.9 * lstat[j, :, 512:] + 0.1 * stat_in[j, 1].astype(F32)
        rstat[j, :, :512] = 0.9 * rstat[j, :, :512] + 0.1 * stat_in[j, 2].astype(F32)
        rstat[j, :, 512:] = 0.9 * rstat[j, :, 512:] + 0.1 * stat_in[j, 3].astype(F32)

    stages = [x_line, z_line, y_line]

    def stage_copies(s):
        return [
            remote(tile.at[s], tiles_in.at[s, n], sem_ts.at[s, n], sem_t.at[s, n], *peer)
            for n, peer in enumerate(stages[s])
        ]

    def start_stage(s):
        for copy in stage_copies(s):
            copy.start()

    def end_stage(s):
        for copy in stage_copies(s):
            copy.wait()
        total = tile[s]
        for n in range(len(stages[s])):
            total += tiles_in[s, n]
        tile[s + 1] = total

    def start_sums():
        tile[0] = jnp.zeros((8, 128), F32)
        tile[0, 0:1, :] = jnp.sum(adam[...].T, axis=0, keepdims=True)
        tile[0, 1:2, :] = jnp.sum(sham[...].T, axis=0, keepdims=True)
        start_stage(0)

    def wait_sent(handled):
        for j in range(3):
            wait_units(12, sem_g1s.at[j])
            wait_units(7, sem_ss.at[j])
            if j in handled:
                wait_units(14, sem_s1s.at[j])
                wait_units(12, sem_gs.at[j])
                wait_units(2, sem_ls.at[j])
                wait_units(4, sem_ps.at[j])
                wait_units(12, sem_qs.at[j])
            else:
                wait_units(16, sem_gs.at[j])
                wait_units(6, sem_rs.at[j])
                wait_units(10, sem_ls.at[j])

    load_blocks.wait()
    load_table.wait()
    pack_grad(0)
    pl.semaphore_wait(barrier, 22)
    send_lines(0)
    send_own(0)
    wait_units(24, sem_in.at[1])
    wait_units(24, sem_in.at[2])

    @pl.when((y + c) % 2 == 0)
    def _():
        send_roots(0, True)
        send_roots(1, False)
        send_roots(2, True)

    @pl.when((y + c) % 2 == 1)
    def _():
        send_roots(0, False)
        send_roots(1, True)

    load_cols.wait()
    load_sec.wait()
    adam[...] = jnp.zeros_like(adam)
    sham[...] = jnp.zeros_like(sham)

    def adam_block(b, carry):
        wide = cols[b].astype(F32)
        new = 0.95 * sec[b] + 0.05 * wide * wide
        sec[b] = new
        value = wide / (jnp.sqrt(new) + 1e-08)
        part = jnp.sum(value * value, axis=0, keepdims=True)
        adam[pl.ds(b, 1), :] = part[:, :128] + part[:, 128:]
        return carry

    load_left.wait()
    load_right.wait()
    pack_grad(1)
    pack_grad(2)
    relay_grad(0)
    lax.fori_loop(0, 64, adam_block, 0)

    @pl.when((y + c) % 2 == 0)
    def _():
        send_lines(1)
        send_own(1)
        fill(0)
        relay_grad(1)
        send_lines(2)
        send_own(2)
        direct(0)
        send_give(0)
        left_up(0)
        left_down(0)
        next_right(0)
        own_left(0)
        own_right(0)
        fill(2)
        relay_grad(2)
        send_mine(0)
        direct(2)
        start_sums()
        send_give(2)
        send_mine(2)
        relay_part(0)
        next_right(2)
        left_down(2)
        relay_part(1)
        end_stage(0)
        start_stage(1)
        own_left(2)
        own_right(2)
        left_up(2)
        relay_part(2)
        end_stage(1)
        start_stage(2)
        receive_up(1)
        receive_down(1)
        end_stage(2)
        wait_sent((0, 2))

    @pl.when((y + c) % 2 == 1)
    def _():
        send_lines(1)
        send_own(1)
        send_roots(2, False)
        fill(1)
        relay_grad(1)
        send_lines(2)
        send_own(2)
        relay_grad(2)
        direct(1)
        start_sums()
        send_give(1)
        send_mine(1)
        left_up(1)
        left_down(1)
        next_right(1)
        relay_part(0)
        own_left(1)
        own_right(1)
        relay_part(1)
        end_stage(0)
        start_stage(1)
        receive_up(0)
        receive_down(0)
        relay_part(2)
        end_stage(1)
        start_stage(2)
        receive_down(2)
        receive_up(2)
        end_stage(2)
        wait_sent((1,))

    sums_out[...] = tile[3]
    wait_units(24, sem_s)


def finish_kernel(slots, lstat, rstat, sec, got, sums, left_out, right_out, second_out, out, wide, rows, sem):
    stores = []
    for n, (src, dst) in enumerate(((lstat, left_out), (rstat, right_out), (sec, second_out))):
        copy = pltpu.make_async_copy(src, dst, sem.at[n])
        copy.start()
        stores.append(copy)

    f = lax.axis_index("fsdp")
    core, x, z = f % 2, (f // 2) % 4, f // 8
    for n in (0, 1):
        rows[n] = jnp.broadcast_to(sums[n : n + 1, :], (128, 128)).T
    for b in range(64):
        rows[2, b : b + 1, :] = rows[1, pl.ds(slots[b], 1), :]
    adam_sq = rows[0, :64] * (1.0 / 1048576.0)
    sham_sq = rows[2, :64] * (1.0 / 1048576.0)
    rows[3, :64] = jnp.sqrt(adam_sq / (sham_sq + 1e-06))

    for b in range(64):
        slot = slots[b]
        j, owner = slot % 3, slot // 3
        c, xs, zs = owner % 2, (owner // 2) % 4, owner // 8
        first = zs + core * (xs - zs)
        rest = (xs - x + core * (zs - z - xs + x) + 8) % 4
        factor = rows[3, b : b + 1, :]
        wide[b, :, :128] = got[j, first, rest, c, :, :128].astype(F32) * factor
        wide[b, :, 128:] = got[j, first, rest, c, :, 128:].astype(F32) * factor
        if b % 16 == 15:
            part = pl.ds(b - 15, 16)
            copy = pltpu.make_async_copy(wide.at[part], out.at[part], sem.at[3 + b // 16])
            copy.start()
            stores.append(copy)
    for copy in stores:
        copy.wait()


def per_device(grad, second, left, right, left_root, right_root, slot_of_block):
    any_space, vmem = pl.BlockSpec(memory_space=pl.ANY), pl.BlockSpec(memory_space=pltpu.VMEM)
    smem = pl.BlockSpec(memory_space=pltpu.SMEM)
    dma = pltpu.SemaphoreType.DMA
    lstat, rstat, sec, got, sums = pl.pallas_call(
        exchange_kernel,
        name="exchange",
        out_shape=(
            pltpu.VMEM((3, 256, 1024), F32),
            pltpu.VMEM((3, 256, 1024), F32),
            pltpu.VMEM((64, 32, 256), F32),
            pltpu.VMEM((3, 4, 4, 2, 32, 256), BF16),
            pltpu.VMEM((8, 128), F32),
        ),
        in_specs=[smem] + [any_space] * 6,
        out_specs=(vmem,) * 5,
        scratch_shapes=[
            pltpu.SMEM((8, 128), jnp.int32),
            pltpu.VMEM((8, 128), jnp.int32),
            pltpu.VMEM((65, 32, 1024), BF16),
            pltpu.VMEM((64, 32, 256), BF16),
            pltpu.VMEM((2, 3, 4, 4, 32, 512), BF16),
            pltpu.VMEM((2, 3, 4, 4, 32, 512), BF16),
            pltpu.VMEM((3, 2, 4, 4, 2, 32, 512), BF16),
            pltpu.VMEM((48, 256, 256), BF16),
            pltpu.VMEM((12, 256, 256), BF16),
            pltpu.VMEM((12, 256, 256), BF16),
            pltpu.VMEM((1024, 512), BF16),
            pltpu.VMEM((3, 2, 4, 4, 32, 256), BF16),
            pltpu.VMEM((3, 2, 4, 4, 32, 256), BF16),
            pltpu.VMEM((2, 3, 4, 4, 32, 256), BF16),
            pltpu.VMEM((3, 4, 256, 512), BF16),
            pltpu.VMEM((3, 4, 256, 512), BF16),
            pltpu.VMEM((128, 128), F32),
            pltpu.VMEM((128, 128), F32),
            pltpu.VMEM((4, 8, 128), F32),
            pltpu.VMEM((3, 7, 8, 128), F32),
            dma((8,)),
            dma((2, 3, 4)), dma((3,)),
            dma((3,)), dma((3,)),
            dma((3,)), dma((3,)),
            dma((3,)), dma((3,)),
            dma((2, 3)), dma((3,)),
            dma, dma((3,)),
            dma((3,)), dma((3,)),
            dma((3,)), dma((3,)),
            dma((3, 7)), dma((3, 7)),
        ],
        compiler_params=pltpu.CompilerParams(
            collective_id=0, has_side_effects=True, vmem_limit_bytes=EXCHANGE_VMEM
        ),
    )(slot_of_block, grad, second, left, right, left_root, right_root)
    return pl.pallas_call(
        finish_kernel,
        name="finish",
        out_shape=(
            jax.ShapeDtypeStruct((3, 256, 1024), F32),
            jax.ShapeDtypeStruct((3, 256, 1024), F32),
            jax.ShapeDtypeStruct((64, 32, 256), F32),
            jax.ShapeDtypeStruct((64, 32, 256), F32),
        ),
        in_specs=[smem] + [vmem] * 5,
        out_specs=(any_space,) * 4,
        scratch_shapes=[pltpu.VMEM((64, 32, 256), F32), pltpu.VMEM((4, 128, 128), F32), dma((7,))],
        compiler_params=pltpu.CompilerParams(vmem_limit_bytes=FINISH_VMEM),
    )(slot_of_block, lstat, rstat, sec, got, sums)


def solution(mesh):
    return jax.shard_map(
        per_device,
        mesh=mesh,
        in_specs=(
            P(None, "fsdp", None),
            P(None, "fsdp", "grp"),
            P("fsdp", "grp", None),
            P("fsdp", "grp", None),
            P("fsdp", "grp", None),
            P("fsdp", "grp", None),
            P(),
        ),
        out_specs=(
            P("fsdp", "grp", None),
            P("fsdp", "grp", None),
            P(None, "fsdp", "grp"),
            P(None, "fsdp", "grp"),
        ),
        check_vma=False,
    )
```

```python
import jax
import jax.numpy as jnp
from jax import lax
from jax.experimental import pallas as pl
from jax.experimental.pallas import tpu as pltpu
from jax.sharding import PartitionSpec as P

MESH = pl.DeviceIdType.MESH
F32, BF16 = jnp.float32, jnp.bfloat16
NT = (((1,), (1,)), ((), ()))
EXCHANGE_VMEM = 50 * 2**20
FINISH_VMEM = 16 * 2**20
SHARE, ROWS, ORDER = 256, 32, 1024


def exchange_kernel(
    slots, grad, second, left, right, left_root, right_root,
    lstat, rstat, sec, got, sums_out,
    table, ranks, blocks, cols, packed, passing, whole, roots, rown, rnext, half,
    mine, give, relayed, stat_out, stat_in, adam, sham, tile, tiles_in,
    sem_in, sem_g1, sem_g1s, sem_g, sem_gs, sem_l, sem_ls, sem_r, sem_rs,
    sem_s1, sem_s1s, sem_s, sem_ss, sem_p, sem_ps, sem_q, sem_qs, sem_t, sem_ts,
):
    f, y = lax.axis_index("fsdp"), lax.axis_index("grp")
    c, x, z = f % 2, (f // 2) % 4, f // 8
    up, down, across = (y + 1 + 2 * c) % 4, (y + 3 + 2 * c) % 4, (y + 2) % 4

    def device(zz, xx, cc):
        return zz * 8 + xx * 2 + cc


    def remote(src, dst, send, recv, ff, yy):
        return pltpu.make_async_remote_copy(
            src_ref=src, dst_ref=dst, send_sem=send, recv_sem=recv, device_id=(ff, yy), device_id_type=MESH
        )

    def move(src, dst, send, recv, ff):
        @pl.when(ff == f)
        def _():
            pltpu.make_async_copy(src, dst, recv).start()

        @pl.when(ff != f)
        def _():
            remote(src, dst, send, recv, ff, y).start()

    def wait_bytes(ref, sem):
        pltpu.make_async_copy(ref, ref, sem).wait()

    def wait_units(n, sem):
        wait_bytes(blocks.at[pl.ds(0, n)], sem)

    x_line = [(device(z, (x + d) % 4, c), y) for d in (1, 2, 3)]
    x_line += [(device(z, (x + d) % 4, 1 - c), y) for d in (0, 1, 2, 3)]
    z_line = [(device((z + d) % 4, x, c), y) for d in (1, 2, 3)]
    z_other = [(device((z + d) % 4, x, 1 - c), y) for d in (1, 2, 3)]
    y_line = [(f, (y + d) % 4) for d in (1, 2, 3)]
    senders = x_line + z_line + z_other + y_line
    senders += [(device(z, (x + d) % 4, c), down) for d in (1, 2, 3)]
    senders += [(device((z + d) % 4, x, c), down) for d in (1, 2, 3)]
    barrier = pltpu.get_barrier_semaphore()
    for peer in senders:
        pl.semaphore_signal(barrier, inc=1, device_id=peer, device_id_type=MESH)

    lane = lax.broadcasted_iota(jnp.int32, (8, 128), 1)
    rank = jnp.full((8, 128), 64, jnp.int32)
    for b in range(64):
        rank = jnp.where(lane == slots[b], b, rank)
    ranks[...] = rank

    def load(src, dst, n):
        copy = pltpu.make_async_copy(src, dst, sem_in.at[n])
        copy.start()
        return copy

    load_blocks = load(grad, blocks.at[pl.ds(0, 64)], 0)
    for j in range(3):
        for k in range(4):
            load(left_root.at[j, :, pl.ds(k * SHARE, SHARE)], roots.at[j * 16 + k * 4 + y], 1)
            load(right_root.at[j, :, pl.ds(k * SHARE, SHARE)], rown.at[j * 4 + k], 2)
    load_table = load(ranks, table, 7)
    load_cols = load(grad.at[:, :, pl.ds(pl.multiple_of(y * SHARE, SHARE), SHARE)], cols, 3)
    load_sec = load(second, sec, 4)
    load_left = load(left, lstat, 5)
    load_right = load(right, rstat, 6)

    blocks[64] = jnp.zeros((ROWS, ORDER), BF16)


    def to_handler(j, route, piece, zs, xs, other):
        cc = (y + j) % 2
        ff = device(other, x, cc) if route == 0 else device(z, other, cc)
        move(piece, whole.at[j, route, zs, xs, c], sem_gs.at[j], sem_g.at[j], ff)

    def pack_grad(j):
        cc = (y + j) % 2

        def pack(n, carry):
            zz, xx = n // 4, n % 4
            piece = blocks[table[0, device(zz, xx, cc) * 3 + j]]
            packed[0, j, xx, zz] = piece[:, :512]
            packed[1, j, zz, xx] = piece[:, 512:]
            return carry

        lax.fori_loop(0, 16, pack, 0)

    def send_lines(j):
        for d in (1, 3, 2):
            xx, zz = (x + d) % 4, (z + d) % 4
            remote(
                packed.at[0, j, xx], passing.at[0, j, x], sem_g1s.at[j], sem_g1.at[0, j, x], device(z, xx, c), y
            ).start()
            remote(
                packed.at[1, j, zz], passing.at[1, j, z], sem_g1s.at[j], sem_g1.at[1, j, z], device(zz, x, c), y
            ).start()

    def send_own(j):
        for d in (1, 3, 2, 0):
            xx, zz = (x + d) % 4, (z + d) % 4
            to_handler(j, 0, packed.at[0, j, x, zz], z, x, zz)
            to_handler(j, 1, packed.at[1, j, z, xx], z, x, xx)

    def relay_grad(j, distances=(1, 3, 2)):
        for e in distances:
            xs, zs = (x + e) % 4, (z + e) % 4
            wait_units(2, sem_g1.at[0, j, xs])
            for d in (1, 3, 2, 0):
                to_handler(j, 0, passing.at[0, j, xs, (z + d) % 4], z, xs, (z + d) % 4)
            wait_units(2, sem_g1.at[1, j, zs])
            for d in (1, 3, 2, 0):
                to_handler(j, 1, passing.at[1, j, zs, (x + d) % 4], zs, x, (x + d) % 4)

    def send_roots(j, handled):
        def block(k, yy):
            at = roots.at[j * 16 + k * 4 + y]
            remote(at, at, sem_ls.at[j], sem_l.at[j], f, yy).start()

        if handled:
            block(y, across)
        else:
            for k in (y, up, across):
                block(k, down)
                at = j * 4 + k
                remote(rown.at[at], rnext.at[at], sem_rs.at[j], sem_r.at[j], f, down).start()
            for k in (y, down):
                block(k, up)

    def fill(j):
        wait_units(12, sem_l.at[j])
        for r, k in ((up, y), (across, y), (down, y), (across, up), (down, up), (across, down)):
            roots[j * 16 + k * 4 + r] = roots[j * 16 + r * 4 + k].T
        rnext[j * 4 + y] = rown[j * 4 + up].T

    def rows_at(j, h, r):
        return whole[j, h, r].reshape(SHARE, 512)

    def direct(j):
        wait_units(6, sem_r.at[j])
        wait_units(32, sem_g.at[j])
        lhs = jnp.concatenate([whole[j, h].reshape(ORDER, 512) for h in (0, 1)], axis=1)
        rhs = jnp.concatenate(
            [jnp.concatenate([root[j * 4 + k] for k in range(4)], axis=1) for root in (rnext, rown)], axis=0
        )
        half[...] = lax.dot_general(lhs, rhs, NT, preferred_element_type=F32).astype(BF16)
        lhs = jnp.concatenate(
            [roots[j * 16 + k * 4 : j * 16 + k * 4 + 4].reshape(ORDER, SHARE) for k in range(4)], axis=1
        )
        value = jnp.dot(lhs, half[...], preferred_element_type=F32)
        for n, out in enumerate((give, mine)):
            piece = value[:, n * SHARE : (n + 1) * SHARE].astype(BF16).reshape(4, 4, 2, ROWS, SHARE)
            out[j, 0] = piece[:, :, 0]
            out[j, 1] = piece[:, :, 1]
        part = jnp.sum(value * value, axis=0, keepdims=True)
        sham[pl.ds(f * 3 + j, 1), :] = part[:, :128] + part[:, 128:256] + part[:, 256:384] + part[:, 384:]

    def send_give(j):
        for d in (1, 3, 2, 0):
            xx, zz = (x + d) % 4, (z + d) % 4
            e = (4 - d) % 4
            remote(
                give.at[j, 0, :, xx], relayed.at[0, j, e], sem_s1s.at[j], sem_s1.at[0, j], device(z, xx, c), up
            ).start()
            remote(
                give.at[j, 1, zz], relayed.at[1, j, e], sem_s1s.at[j], sem_s1.at[1, j], device(zz, x, c), up
            ).start()

    def send_mine(j):
        for d in (1, 3, 2):
            xx, zz = (x + d) % 4, (z + d) % 4
            remote(
                mine.at[j, 0, :, xx], relayed.at[0, j, 4 - d], sem_s1s.at[j], sem_s1.at[0, j], device(z, xx, c), y
            ).start()
            remote(
                mine.at[j, 1, zz], relayed.at[1, j, 4 - d], sem_s1s.at[j], sem_s1.at[1, j], device(zz, x, c), y
            ).start()
        pltpu.make_async_copy(mine.at[j, 0, :, x], relayed.at[0, j, 0], sem_s1.at[0, j]).start()
        pltpu.make_async_copy(mine.at[j, 1, z], relayed.at[1, j, 0], sem_s1.at[1, j]).start()

    def relay_part(j):
        wait_units(4, sem_s1.at[0, j])
        for d in (1, 3, 2, 0):
            zz = (z + d) % 4
            move(relayed.at[0, j, :, zz], got.at[j, z, :, c], sem_ss.at[j], sem_s, device(zz, x, 0))
        wait_units(4, sem_s1.at[1, j])
        for d in (1, 3, 2, 0):
            xx = (x + d) % 4
            move(relayed.at[1, j, :, xx], got.at[j, x, :, c], sem_ss.at[j], sem_s, device(z, xx, 1))

    def left_part(j, r, h):
        value = lax.dot_general(
            rows_at(j, 0, r), whole[j, 0, 2 * h : 2 * h + 2].reshape(512, 512), NT, preferred_element_type=F32
        )
        value += lax.dot_general(
            rows_at(j, 1, r), whole[j, 1, 2 * h : 2 * h + 2].reshape(512, 512), NT, preferred_element_type=F32
        )
        return value

    def right_parts(j, r):
        at = pl.ds(pl.multiple_of((r % 2) * SHARE, SHARE), SHARE)
        lhs = whole[j, r // 2, :, :, :, :, at].reshape(ORDER, SHARE).T
        return [jnp.dot(lhs, whole[j, h].reshape(ORDER, 512), preferred_element_type=F32) for h in (0, 1)]

    def left_up(j):
        stat_out[j, 0] = left_part(j, up, 0).astype(BF16)
        remote(stat_out.at[j, 0], stat_in.at[j, 0], sem_ps.at[j], sem_p.at[j], f, up).start()

    def left_down(j):
        stat_out[j, 1] = left_part(j, down, 1).astype(BF16)
        remote(stat_out.at[j, 1], stat_in.at[j, 1], sem_qs.at[j], sem_q.at[j], f, down).start()

    def next_right(j):
        both = pl.ds(2, 2)
        for h, value in enumerate(right_parts(j, down)):
            stat_out[j, 2 + h] = value.astype(BF16)
        remote(stat_out.at[j, both], stat_in.at[j, both], sem_qs.at[j], sem_q.at[j], f, down).start()

    def own_left(j):
        for h in (0, 1):
            at = slice(h * 512, (h + 1) * 512)
            lstat[j, :, at] = 0.9 * lstat[j, :, at] + 0.1 * left_part(j, y, h)

    def own_right(j):
        for h, value in enumerate(right_parts(j, y)):
            at = slice(h * 512, (h + 1) * 512)
            rstat[j, :, at] = 0.9 * rstat[j, :, at] + 0.1 * value

    def receive_up(j):
        wait_units(4, sem_p.at[j])
        lstat[j, :, :512] = 0.9 * lstat[j, :, :512] + 0.1 * stat_in[j, 0].astype(F32)

    def receive_down(j):
        wait_units(12, sem_q.at[j])
        lstat[j, :, 512:] = 0.9 * lstat[j, :, 512:] + 0.1 * stat_in[j, 1].astype(F32)
        rstat[j, :, :512] = 0.9 * rstat[j, :, :512] + 0.1 * stat_in[j, 2].astype(F32)
        rstat[j, :, 512:] = 0.9 * rstat[j, :, 512:] + 0.1 * stat_in[j, 3].astype(F32)

    stages = [x_line, z_line, y_line]

    def stage_copies(s):
        return [
            remote(tile.at[s], tiles_in.at[s, n], sem_ts.at[s, n], sem_t.at[s, n], *peer)
            for n, peer in enumerate(stages[s])
        ]

    def start_stage(s):
        for copy in stage_copies(s):
            copy.start()

    def end_stage(s):
        for copy in stage_copies(s):
            copy.wait()
        total = tile[s]
        for n in range(len(stages[s])):
            total += tiles_in[s, n]
        tile[s + 1] = total

    def start_sums():
        tile[0] = jnp.zeros((8, 128), F32)
        tile[0, 0:1, :] = jnp.sum(adam[...].T, axis=0, keepdims=True)
        tile[0, 1:2, :] = jnp.sum(sham[...].T, axis=0, keepdims=True)
        start_stage(0)

    def wait_sent(handled):
        for j in range(3):
            wait_units(12, sem_g1s.at[j])
            wait_units(7, sem_ss.at[j])
            if j in handled:
                wait_units(14, sem_s1s.at[j])
                wait_units(12, sem_gs.at[j])
                wait_units(2, sem_ls.at[j])
                wait_units(4, sem_ps.at[j])
                wait_units(12, sem_qs.at[j])
            else:
                wait_units(16, sem_gs.at[j])
                wait_units(6, sem_rs.at[j])
                wait_units(10, sem_ls.at[j])

    load_blocks.wait()
    load_table.wait()
    pack_grad(0)
    pl.semaphore_wait(barrier, 22)
    send_lines(0)
    send_own(0)
    wait_units(24, sem_in.at[1])
    wait_units(24, sem_in.at[2])

    @pl.when((y + c) % 2 == 0)
    def _():
        send_roots(0, True)
        send_roots(1, False)
        send_roots(2, True)

    @pl.when((y + c) % 2 == 1)
    def _():
        send_roots(0, False)
        send_roots(1, True)

    load_cols.wait()
    load_sec.wait()
    adam[...] = jnp.zeros_like(adam)
    sham[...] = jnp.zeros_like(sham)

    def adam_block(b, carry):
        wide = cols[b].astype(F32)
        new = 0.95 * sec[b] + 0.05 * wide * wide
        sec[b] = new
        value = wide / (jnp.sqrt(new) + 1e-08)
        part = jnp.sum(value * value, axis=0, keepdims=True)
        adam[pl.ds(b, 1), :] = part[:, :128] + part[:, 128:]
        return carry

    load_left.wait()
    load_right.wait()
    pack_grad(1)
    pack_grad(2)
    relay_grad(0)
    lax.fori_loop(0, 64, adam_block, 0)

    @pl.when((y + c) % 2 == 0)
    def _():
        send_lines(1)
        send_own(1)
        fill(0)
        direct(0)
        send_give(0)
        relay_grad(1)
        send_lines(2)
        send_own(2)
        left_up(0)
        left_down(0)
        next_right(0)
        own_left(0)
        own_right(0)
        fill(2)
        relay_grad(2)
        send_mine(0)
        direct(2)
        start_sums()
        send_give(2)
        send_mine(2)
        relay_part(0)
        next_right(2)
        left_down(2)
        relay_part(1)
        end_stage(0)
        start_stage(1)
        own_left(2)
        own_right(2)
        left_up(2)
        relay_part(2)
        end_stage(1)
        start_stage(2)
        receive_up(1)
        receive_down(1)
        end_stage(2)
        wait_sent((0, 2))

    @pl.when((y + c) % 2 == 1)
    def _():
        send_lines(1)
        send_own(1)
        send_roots(2, False)
        fill(1)
        relay_grad(1)
        send_lines(2)
        send_own(2)
        relay_grad(2)
        direct(1)
        start_sums()
        send_give(1)
        send_mine(1)
        left_up(1)
        left_down(1)
        next_right(1)
        relay_part(0)
        own_left(1)
        own_right(1)
        relay_part(1)
        end_stage(0)
        start_stage(1)
        receive_up(0)
        receive_down(0)
        relay_part(2)
        end_stage(1)
        start_stage(2)
        receive_down(2)
        receive_up(2)
        end_stage(2)
        wait_sent((1,))

    sums_out[...] = tile[3]
    wait_units(24, sem_s)


def finish_kernel(slots, lstat, rstat, sec, got, sums, left_out, right_out, second_out, out, wide, rows, sem):
    stores = []
    for n, (src, dst) in enumerate(((lstat, left_out), (rstat, right_out), (sec, second_out))):
        copy = pltpu.make_async_copy(src, dst, sem.at[n])
        copy.start()
        stores.append(copy)

    f = lax.axis_index("fsdp")
    core, x, z = f % 2, (f // 2) % 4, f // 8
    for n in (0, 1):
        rows[n] = jnp.broadcast_to(sums[n : n + 1, :], (128, 128)).T
    for b in range(64):
        rows[2, b : b + 1, :] = rows[1, pl.ds(slots[b], 1), :]
    adam_sq = rows[0, :64] * (1.0 / 1048576.0)
    sham_sq = rows[2, :64] * (1.0 / 1048576.0)
    rows[3, :64] = jnp.sqrt(adam_sq / (sham_sq + 1e-06))

    for b in range(64):
        slot = slots[b]
        j, owner = slot % 3, slot // 3
        c, xs, zs = owner % 2, (owner // 2) % 4, owner // 8
        first = zs + core * (xs - zs)
        rest = (xs - x + core * (zs - z - xs + x) + 8) % 4
        factor = rows[3, b : b + 1, :]
        wide[b, :, :128] = got[j, first, rest, c, :, :128].astype(F32) * factor
        wide[b, :, 128:] = got[j, first, rest, c, :, 128:].astype(F32) * factor
        if b % 16 == 15:
            part = pl.ds(b - 15, 16)
            copy = pltpu.make_async_copy(wide.at[part], out.at[part], sem.at[3 + b // 16])
            copy.start()
            stores.append(copy)
    for copy in stores:
        copy.wait()


def per_device(grad, second, left, right, left_root, right_root, slot_of_block):
    any_space, vmem = pl.BlockSpec(memory_space=pl.ANY), pl.BlockSpec(memory_space=pltpu.VMEM)
    smem = pl.BlockSpec(memory_space=pltpu.SMEM)
    dma = pltpu.SemaphoreType.DMA
    lstat, rstat, sec, got, sums = pl.pallas_call(
        exchange_kernel,
        name="exchange",
        out_shape=(
            pltpu.VMEM((3, 256, 1024), F32),
            pltpu.VMEM((3, 256, 1024), F32),
            pltpu.VMEM((64, 32, 256), F32),
            pltpu.VMEM((3, 4, 4, 2, 32, 256), BF16),
            pltpu.VMEM((8, 128), F32),
        ),
        in_specs=[smem] + [any_space] * 6,
        out_specs=(vmem,) * 5,
        scratch_shapes=[
            pltpu.SMEM((8, 128), jnp.int32),
            pltpu.VMEM((8, 128), jnp.int32),
            pltpu.VMEM((65, 32, 1024), BF16),
            pltpu.VMEM((64, 32, 256), BF16),
            pltpu.VMEM((2, 3, 4, 4, 32, 512), BF16),
            pltpu.VMEM((2, 3, 4, 4, 32, 512), BF16),
            pltpu.VMEM((3, 2, 4, 4, 2, 32, 512), BF16),
            pltpu.VMEM((48, 256, 256), BF16),
            pltpu.VMEM((12, 256, 256), BF16),
            pltpu.VMEM((12, 256, 256), BF16),
            pltpu.VMEM((1024, 512), BF16),
            pltpu.VMEM((3, 2, 4, 4, 32, 256), BF16),
            pltpu.VMEM((3, 2, 4, 4, 32, 256), BF16),
            pltpu.VMEM((2, 3, 4, 4, 32, 256), BF16),
            pltpu.VMEM((3, 4, 256, 512), BF16),
            pltpu.VMEM((3, 4, 256, 512), BF16),
            pltpu.VMEM((128, 128), F32),
            pltpu.VMEM((128, 128), F32),
            pltpu.VMEM((4, 8, 128), F32),
            pltpu.VMEM((3, 7, 8, 128), F32),
            dma((8,)),
            dma((2, 3, 4)), dma((3,)),
            dma((3,)), dma((3,)),
            dma((3,)), dma((3,)),
            dma((3,)), dma((3,)),
            dma((2, 3)), dma((3,)),
            dma, dma((3,)),
            dma((3,)), dma((3,)),
            dma((3,)), dma((3,)),
            dma((3, 7)), dma((3, 7)),
        ],
        compiler_params=pltpu.CompilerParams(
            collective_id=0, has_side_effects=True, vmem_limit_bytes=EXCHANGE_VMEM
        ),
    )(slot_of_block, grad, second, left, right, left_root, right_root)
    return pl.pallas_call(
        finish_kernel,
        name="finish",
        out_shape=(
            jax.ShapeDtypeStruct((3, 256, 1024), F32),
            jax.ShapeDtypeStruct((3, 256, 1024), F32),
            jax.ShapeDtypeStruct((64, 32, 256), F32),
            jax.ShapeDtypeStruct((64, 32, 256), F32),
        ),
        in_specs=[smem] + [vmem] * 5,
        out_specs=(any_space,) * 4,
        scratch_shapes=[pltpu.VMEM((64, 32, 256), F32), pltpu.VMEM((4, 128, 128), F32), dma((7,))],
        compiler_params=pltpu.CompilerParams(vmem_limit_bytes=FINISH_VMEM),
    )(slot_of_block, lstat, rstat, sec, got, sums)


def solution(mesh):
    return jax.shard_map(
        per_device,
        mesh=mesh,
        in_specs=(
            P(None, "fsdp", None),
            P(None, "fsdp", "grp"),
            P("fsdp", "grp", None),
            P("fsdp", "grp", None),
            P("fsdp", "grp", None),
            P("fsdp", "grp", None),
            P(),
        ),
        out_specs=(
            P("fsdp", "grp", None),
            P("fsdp", "grp", None),
            P(None, "fsdp", "grp"),
            P(None, "fsdp", "grp"),
        ),
        check_vma=False,
    )
```
